512 devices in a mesh: dp: 32 (over y, x), expert: 16 (over z, core).
Axes of the slice: x: 4, y: 8, z: 8, core: 2. Of those that a mesh axis runs over, the one named last changes fastest.
Arguments:
- tokens: bfloat16 [1024, 7168], P(('dp', 'expert')), may hold values from -6 to 6
- w_gate: bfloat16 [16, 7168, 1024], P('expert', 'dp'), may hold values from -0.0625 to 0.0625
- w_up: bfloat16 [16, 7168, 1024], P('expert', 'dp'), may hold values from -0.0625 to 0.0625
- w_down: bfloat16 [16, 1024, 7168], P('expert', None, 'dp'), may hold values from -0.1875 to 0.1875
- routes: int32 [1024, 8], P(('dp', 'expert')), may hold values from 0 to 15, all different within a row; in each aligned block of 2 rows (0 to 1, 2 to 3, ...) at most 2 rows name the same one
- scores: float32 [1024, 8], P(('dp', 'expert')), may hold values from 0.1 to 1
Outputs:
- mixed: bfloat16 [1024, 7168], P(('dp', 'expert'))
The draws below stay inside these ranges and needn't reach their ends.
Inputs may be any that keep to these rules, and one draw needn't show every extreme that they name: `routes`: in the rows of one device no expert is named more than 2 times, a bound that some block reaches there; a request names 8 different experts.
All inputs are finite; a program needn't handle non-finite values.
Results may differ from the reference program's by a relative error of at most 0.034.
Values may be sent and summed in bfloat16 or wider, within the bound.
A program may use at most 64 MiB of HBM per device.

```python
import math
import jax
import jax.numpy as jnp
import numpy as np
from jax import lax

D = 7168
FFW = 1024
REQ_DEV = 2
EXPERTS = 16
TOPK = 8
CAP = 2
REQUESTS = 1024
N_DP = 32
N_EXPERT = 16


def steps_of(stream_key, dims, cuts, low, top_value):
    factor_of, own = 1.0, jax.random.fold_in(stream_key, 6)
    for axis_at, blocks in cuts:
        draws = jnp.exp(jax.random.uniform(jax.random.fold_in(own, axis_at), (blocks,), jnp.float32, low / len(cuts), top_value / len(cuts)))
        factor_of = factor_of * jnp.repeat(draws, dims[axis_at] // blocks).reshape([-1 if axis == axis_at else 1 for axis in range(len(dims))])
    return factor_of


def deal_out(stream_key, own, number, rows, number_of, top, limit, lean):
    ranking = jax.random.permutation(stream_key, number_of)
    heavy_load, common = portions_of(number_of, rows * top, limit, lean, True), portions_of(number_of, rows * top, limit, lean, False)
    places = jnp.arange(number_of)

    def named(sizes, turn):
        used = int((sizes > 0).sum())
        fixed = max(1, used // 4)
        moved = fixed + (places - fixed + turn * (used - fixed)) % max(1, number_of - fixed)
        return jnp.zeros((number_of,), jnp.int32).at[ranking[jnp.where(places < fixed, places, moved)]].set(jnp.asarray(sizes, jnp.int32))

    sizes = jnp.where(number % 4 == 0, named(heavy_load, number // 4), named(common, number - number // 4 - 1))
    mixed = jax.random.permutation(jax.random.fold_in(own, 3), number_of)
    source_of, taker = mixed[0:number_of // 2 * 2:2], mixed[1:number_of // 2 * 2:2]
    slack = jnp.minimum(sizes[source_of] - 1, limit - sizes[taker]) // 2
    slack = jnp.where((source_of == ranking[0]) | (taker == ranking[0]) | (sizes[taker] == 0), 0, jnp.maximum(slack, 0))
    moved = jax.random.randint(jax.random.fold_in(own, 4), (number_of // 2,), 0, 1 << 20) % (slack + 1)
    sizes = sizes.at[source_of].add(-moved).at[taker].add(moved)
    items = jnp.searchsorted(jnp.cumsum(sizes), jnp.arange(rows * top), side="right").astype(jnp.int32)
    table = items.reshape(top, rows).T
    table = table[jax.random.permutation(jax.random.fold_in(own, 1), rows)]
    turn = jax.random.randint(jax.random.fold_in(own, 2), (rows, 1), 0, top)
    return jnp.take_along_axis(table, (jnp.arange(top)[None, :] + turn) % top, axis=1)


def portions_of(count, total, reach, lean, full):
    weights = [(1 << 20) // math.isqrt(grade ** lean) + 1 for grade in range(1, count + 1)]
    largest = reach if full else min(reach, max(-(-total // count), total * weights[0] // sum(weights)))
    least = 1 if total - largest >= count - 1 else 0
    given, rest = [largest] + [least] * (count - 1), total - largest - least * (count - 1)
    while rest > 0:
        candidates = [i for i in range(1, count) if given[i] < largest] or [i for i in range(1, count) if given[i] < reach]
        whole, remaining = sum([weights[i] for i in candidates]), rest
        for i in candidates:
            extra = min(reach - given[i], max(1, remaining * weights[i] // whole), rest)
            given[i] = given[i] + extra
            rest = rest - extra
    return np.array(given)


def bell_draw(own_key, extent, spread, bound, cuts=(), kind=jnp.bfloat16):
    entries = jax.random.normal(own_key, extent, jnp.float32) * spread
    if len(cuts) > 0:
        entries = steps_of(own_key, extent, cuts, -0.22, 0.18) * entries
    return jnp.clip(entries, min=-bound, max=bound).astype(kind)


def setup_inputs(seed: int = 0) -> dict:
    keys = jax.random.split(jax.random.key(seed), 7)
    tokens = bell_draw(keys[0], (REQUESTS, D), 1.0, 6.0, ((0, 512),))
    w_gate = bell_draw(keys[1], (EXPERTS, D, FFW), D ** -0.5, 0.0625, ((0, 16), (1, 32)))
    w_up = bell_draw(keys[2], (EXPERTS, D, FFW), D ** -0.5, 0.0625, ((0, 16), (1, 32)))
    w_down = bell_draw(keys[3], (EXPERTS, FFW, D), FFW ** -0.5, 0.1875, ((0, 16), (2, 32)))
    routes_keys = jax.random.split(jax.random.fold_in(keys[4], 1), REQUESTS // REQ_DEV)
    routes_turns = jax.random.permutation(jax.random.fold_in(keys[4], 3), REQUESTS // REQ_DEV)
    routes = jax.vmap(lambda own, number: deal_out(jax.random.fold_in(keys[4], 2), own, number, REQ_DEV, EXPERTS, TOPK, CAP, 2))(routes_keys, routes_turns).reshape((REQUESTS, TOPK))
    scores = jnp.clip(jnp.exp(math.log(1.0) - 2.3025851 * jax.random.uniform(keys[5], (REQUESTS, TOPK), jnp.float32) ** steps_of(keys[5], (REQUESTS, TOPK), ((0, 512),), -0.2, 0.2)), 0.1, 1.0)
    return dict(tokens=tokens, w_gate=w_gate, w_up=w_up, w_down=w_down, routes=routes, scores=scores)


route_scale = 2.5


def summed_partials(pieces, weight):
    slice_width = pieces.shape[2]
    blocks = weight.reshape(N_DP, slice_width, weight.shape[1]).astype(jnp.float32)
    partial_value = jnp.einsum("mbd,bdf->bmf", pieces, blocks)
    rounded = lax.optimization_barrier(partial_value.astype(jnp.bfloat16)).astype(jnp.float32)
    return jnp.sum(rounded, axis=0)


def reference(tokens, w_gate, w_up, w_down, routes, scores):
    devices = N_DP * N_EXPERT
    width = tokens.shape[1]
    slice_width = width // N_DP
    per_device = routes.reshape(devices, REQ_DEV * TOPK)
    hits = (per_device[:, :, None] == jnp.arange(EXPERTS, dtype=jnp.int32)[None, None, :]).astype(jnp.int32)
    before = jnp.cumsum(hits, axis=1) - hits
    position = jnp.sum(before * hits, axis=2).astype(jnp.int32)
    sources = jnp.arange(devices, dtype=jnp.int32)[:, None]
    targets = (per_device * (devices * CAP) + sources * CAP + position).reshape(-1).astype(jnp.int32)
    repeated = jnp.repeat(tokens, TOPK, axis=0)
    dispatched = jnp.zeros((EXPERTS * devices * CAP, width), jnp.bfloat16).at[targets].set(repeated)
    dispatched = dispatched.reshape(EXPERTS, devices * CAP, width)

    def one_expert(operands):
        slot_rows, gate_w, up_w, down_w = operands
        pieces = slot_rows.reshape(slot_rows.shape[0], N_DP, slice_width).astype(jnp.float32)
        gate = summed_partials(pieces, gate_w)
        upper = summed_partials(pieces, up_w)
        hidden = (jax.nn.silu(gate) * upper).astype(jnp.bfloat16)
        return jnp.dot(hidden, down_w, preferred_element_type=jnp.float32).astype(jnp.bfloat16)

    expert_out = lax.map(one_expert, (dispatched, w_gate, w_up, w_down))
    picked = jnp.take(expert_out.reshape(-1, width), targets, axis=0)
    picked = picked.reshape(tokens.shape[0], TOPK, width).astype(jnp.float32)
    weights = route_scale * scores / jnp.sum(scores, axis=1, keepdims=True)
    combined = jnp.einsum("rk,rkd->rd", weights, picked)
    return combined.astype(jnp.bfloat16)
```

```python
import functools

import jax
import jax.numpy as jnp
from jax import lax
from jax.experimental import pallas as pl
from jax.experimental.pallas import tpu as pltpu
from jax.sharding import PartitionSpec as P

MESH = pl.DeviceIdType.MESH
F32 = jnp.float32
BF16 = jnp.bfloat16

ROUTE_SCALE = 2.5
NX, NY, NZ = 4, 8, 8
N_DP = NX * NY
N_EXPERT = 2 * NZ
D = 7168
WIDTH = D // N_DP
FFW = 1024
PAD = 256
ROWS = 64
CHUNK = 2 * ROWS
QUARTER = FFW // NX
STRIP = CHUNK // NY
OFFSETS = (0, 1, 7, 2, 6, 3, 5, 4)
BACK = tuple(OFFSETS.index((NZ - o) % NZ) for o in OFFSETS)
STAGGER = 1


def kernel(
    tok_ref, wg_hbm, wu_hbm, wd_hbm, out_ref,
    wg, wu, wd, mail, xall, part, xa, xy, xs, ya, yt, yx, hid, outs, got, back_src, back,
    load_sem, mail_sem, x_send, x_recv, rs_send, rs_recv, ag_send, ag_recv, o_send, o_recv, b_sem,
):
    dp = lax.axis_index("dp")
    e = lax.axis_index("expert")
    X, Y = dp % NX, dp // NX
    Z, C = e // 2, e % 2

    def at(x, y):
        return (lax.rem(y, NY) * NX + lax.rem(x, NX), e)

    loads = [
        pltpu.make_async_copy(wg_hbm.at[0], wg.at[pl.ds(0, WIDTH)], load_sem.at[0]),
        pltpu.make_async_copy(wu_hbm.at[0], wu.at[pl.ds(0, WIDTH)], load_sem.at[1]),
        pltpu.make_async_copy(wd_hbm.at[0], wd, load_sem.at[2]),
    ]
    for load in loads:
        load.start()

    barrier = pltpu.get_barrier_semaphore()

    def greet_dp(j, carry):
        pl.semaphore_signal(barrier, inc=1, device_id=((dp + j) % N_DP, e), device_id_type=MESH)
        return carry

    def greet_expert(j, carry):
        pl.semaphore_signal(barrier, inc=1, device_id=(dp, (e + j) % N_EXPERT), device_id_type=MESH)
        return carry

    lax.fori_loop(1, N_DP, greet_dp, 0)
    lax.fori_loop(1, N_EXPERT, greet_expert, 0)

    wg[pl.ds(WIDTH, PAD - WIDTH), :] = jnp.zeros((PAD - WIDTH, FFW), BF16)
    wu[pl.ds(WIDTH, PAD - WIDTH), :] = jnp.zeros((PAD - WIDTH, FFW), BF16)
    outs[...] = jnp.zeros_like(outs)

    pl.semaphore_wait(barrier, N_DP - 1 + N_EXPERT - 1)

    sends = []

    def send(src, dst, send_sem, recv_sem, device):
        copy = pltpu.make_async_remote_copy(src, dst, send_sem, recv_sem, device_id=device, device_id_type=MESH)
        copy.start()
        sends.append(copy)
        return copy

    def spread(src, dst, sems):
        own = pltpu.make_async_copy(src.at[dp], dst.at[dp], sems.at[1])
        own.start()

        def body(j, carry):
            d = (dp + j) % N_DP
            pltpu.make_async_remote_copy(
                src.at[d], dst.at[dp], sems.at[0], sems.at[1], device_id=(d, e), device_id_type=MESH
            ).start()
            return carry

        lax.fori_loop(1, N_DP, body, 0)
        pltpu.make_async_copy(src, dst, sems.at[1]).wait()

    def spread_done(src, dst, sems):
        pltpu.make_async_copy(src.at[pl.ds(0, N_DP - 1)], dst.at[pl.ds(0, N_DP - 1)], sems.at[0]).wait()

    spread(tok_ref, mail, mail_sem)
    m = lax.broadcasted_iota(jnp.int32, (CHUNK, N_DP * 8), 0)
    n = lax.broadcasted_iota(jnp.int32, (CHUNK, N_DP * 8), 1)
    row = m & (ROWS - 1)
    pick = ((row >> 1) * 8 + (row & 1) * 2 + (m >> 6) == n).astype(BF16)
    halves = jnp.dot(pick, mail[...].reshape(N_DP * 8, 128).astype(BF16), preferred_element_type=F32)
    xall[e] = jnp.concatenate([halves[:ROWS], halves[ROWS:]], axis=1).astype(BF16)

    x_copies = {}
    for k, off in enumerate(OFFSETS):
        for c in range(2):
            if k == 0 and c == 0:
                continue
            target = ((Z + off) % NZ) * 2 + (C + c) % 2
            x_copies[BACK[k], c] = send(
                xall.at[e], xall.at[e], x_send.at[k, c], x_recv.at[BACK[k], c], (dp, target)
            )

    for load in loads:
        load.wait()

    def add(ref, value):
        ref[...] = (ref[...].astype(F32) + value.astype(F32)).astype(BF16)

    def x_stage(k, s, piece, buf, base):
        c1 = send(piece(X + 2), buf.at[0], rs_send.at[k, base], rs_recv.at[k, base], at(X + s + NX, Y))
        c2 = send(
            piece(X - s + NX), buf.at[1], rs_send.at[k, base + 1], rs_recv.at[k, base + 1], at(X - s + NX, Y)
        )
        yield
        c1.wait_recv()
        add(buf.at[0], piece(X + s + NX)[...])
        c3 = send(buf.at[0], buf.at[2], rs_send.at[k, base + 2], rs_recv.at[k, base + 2], at(X + s + NX, Y))
        yield
        c2.wait_recv()
        c3.wait_recv()
        return piece(X)[...].astype(F32) + buf[1].astype(F32) + buf[2].astype(F32)

    def y_stage(k, s, piece, buf, base):
        up, down = at(X, Y + s + NY), at(X, Y - s + NY)
        a = b = None
        for step in range(4):
            src = piece(Y + 4) if step == 0 else buf.at[step - 1]
            if step > 0:
                a.wait_recv()
                add(src, piece(Y + (4 - step) * s + NY)[...])
            a = send(src, buf.at[step], rs_send.at[k, base + step], rs_recv.at[k, base + step], up)
            if step < 3:
                src = piece(Y - 3 * s + NY) if step == 0 else buf.at[3 + step]
                if step > 0:
                    b.wait_recv()
                    add(src, piece(Y - (3 - step) * s + NY)[...])
                b = send(
                    src, buf.at[4 + step], rs_send.at[k, base + 4 + step], rs_recv.at[k, base + 4 + step], down
                )
            yield
        a.wait_recv()
        b.wait_recv()
        return piece(Y)[...].astype(F32) + buf[3].astype(F32) + buf[6].astype(F32)

    def strip_at(y):
        return pl.ds(pl.multiple_of(lax.rem(y, NY) * STRIP, STRIP), STRIP)

    def ag_y(k, s, strip, base):
        up, down = at(X, Y + s + NY), at(X, Y - s + NY)
        a = b = None
        for step in range(4):
            if step > 0:
                a.wait_recv()
            ref = strip(Y - step * s + NY)
            a = send(ref, ref, ag_send.at[k, base + step], ag_recv.at[k, base + step], up)
            if step < 3:
                if step > 0:
                    b.wait_recv()
                ref = strip(Y + step * s + NY)
                b = send(ref, ref, ag_send.at[k, base + 4 + step], ag_recv.at[k, base + 4 + step], down)
            yield
        a.wait_recv()
        b.wait_recv()

    def ag_x(k, block, half, base):
        a = send(block(X), block(X), ag_send.at[k, base], ag_recv.at[k, base], at(X + 1, Y))
        b = send(block(X), block(X), ag_send.at[k, base + 1], ag_recv.at[k, base + 1], at(X + NX - 1, Y))
        yield
        a.wait_recv()
        ref = half(X + NX - 1, 0)
        c = send(ref, ref, ag_send.at[k, base + 2], ag_recv.at[k, base + 2], at(X + 1, Y))
        b.wait_recv()
        ref = half(X + 1, 1)
        d = send(ref, ref, ag_send.at[k, base + 3], ag_recv.at[k, base + 3], at(X + NX - 1, Y))
        yield
        c.wait_recv()
        d.wait_recv()

    lane = lax.broadcasted_iota(jnp.int32, (CHUNK, PAD), 1)
    mine = (lane == WIDTH + e) | (lane == WIDTH + N_EXPERT + e)

    def chunk(k):
        off = OFFSETS[k]
        s = 1 if (k // 2) % 2 == 0 else -1
        zc = (Z + off) % NZ
        for c in range(2):
            if (k, c) in x_copies:
                x_copies[k, c].wait_recv()
        x = xall[pl.ds(2 * zc, 2)].reshape(CHUNK, PAD)
        for q in range(NX):
            cols = pl.ds(q * QUARTER, QUARTER)
            part[k, q, :, 0:QUARTER] = jnp.dot(x, wg[:, cols], preferred_element_type=F32).astype(BF16)
            part[k, q, :, QUARTER:] = jnp.dot(x, wu[:, cols], preferred_element_type=F32).astype(BF16)
        i = k // 2
        if k % 2 == 0:
            total = yield from x_stage(k, s, lambda q: part.at[k, lax.rem(q, NX)], xa.at[i], 0)
            xs[i] = total.astype(BF16)
            total = yield from y_stage(k, s, lambda y: xs.at[i, strip_at(y)], xy.at[i], 3)
        else:
            total = yield from y_stage(k, s, lambda y: part.at[k, :, strip_at(y)], ya.at[i], 3)
            yt[i] = total.astype(BF16)
            total = yield from x_stage(k, s, lambda q: yt.at[i, lax.rem(q, NX)], yx.at[i], 0)
        gate, up = total[:, :QUARTER], total[:, QUARTER:]
        hid[k, X, strip_at(Y)] = (gate / (1.0 + jnp.exp(-gate)) * up).astype(BF16)
        if k % 2 == 0:
            half = STRIP // 2
            yield from ag_y(k, s, lambda y: hid.at[k, X, strip_at(y)], 0)
            half = CHUNK // 2
            yield from ag_x(
                k, lambda q: hid.at[k, lax.rem(q, NX)],
                lambda q, h: hid.at[k, lax.rem(q, NX), pl.ds(h * half, half)], 7,
            )
        else:
            def third(q, h):
                return hid.at[k, lax.rem(q, NX), strip_at(Y), pl.ds(h * 128, 128)]

            yield from ag_x(k, lambda q: hid.at[k, lax.rem(q, NX), strip_at(Y)], third, 7)
            yield from ag_y(k, s, lambda y: hid.at[k, :, strip_at(y)], 0)
        o = jnp.dot(hid[k, 0], wd[0:QUARTER, :], preferred_element_type=F32)
        for q in range(1, NX):
            o += jnp.dot(hid[k, q], wd[q * QUARTER:(q + 1) * QUARTER, :], preferred_element_type=F32)
        x = xall[pl.ds(2 * zc, 2)].reshape(CHUNK, PAD)
        weight = jnp.sum(jnp.where(mine, x.astype(F32), 0.0), axis=1, keepdims=True)
        outs[k, :, 0:WIDTH] = (o * weight).astype(BF16)
        for c in range(2):
            target = (C + c) % 2
            rows = outs.at[k, pl.ds(pl.multiple_of(target * ROWS, ROWS), ROWS)]
            if k == 0 and c == 0:
                got[0] = rows[...]
                continue
            o_copies[BACK[k], c] = send(
                rows, got.at[2 * BACK[k] + c], o_send.at[k, c], o_recv.at[BACK[k], c], (dp, zc * 2 + target)
            )

    o_copies = {}
    waiting = [chunk(k) for k in range(NZ)]
    live, slot = [], 0
    while waiting or live:
        if waiting and slot % STAGGER == 0:
            live.append(waiting.pop(0))
        still = []
        for g in live:
            try:
                next(g)
                still.append(g)
            except StopIteration:
                pass
        live = still
        slot += 1

    for key in sorted(o_copies):
        o_copies[key].wait_recv()
    total = got[0].astype(F32)
    for t in range(1, 2 * NZ):
        total += got[t].astype(F32)
    total = total.astype(BF16)
    stacked = jnp.concatenate([total[:, :128], total[:, 128:]], axis=0)
    t = lax.broadcasted_iota(jnp.int32, (N_DP * 8, CHUNK), 0)
    n = lax.broadcasted_iota(jnp.int32, (N_DP * 8, CHUNK), 1)
    sub = t & 7
    place = ((sub < 4) & ((sub & 1) * ROWS + (t >> 3) * 2 + (sub >> 1) == n)).astype(BF16)
    back_src[...] = jnp.dot(place, stacked, preferred_element_type=F32).reshape(N_DP, 8, 128)
    spread(back_src, back, b_sem)
    out_ref[...] = back[...]
    spread_done(tok_ref, mail, mail_sem)
    spread_done(back_src, back, b_sem)
    for copy in sends:
        copy.wait_send()


def shards(tokens, w_gate, w_up, w_down, routes, scores):
    rows = tokens.shape[0]
    weights = ROUTE_SCALE * scores / jnp.sum(scores, axis=1, keepdims=True)
    named = routes[:, :, None] == jnp.arange(N_EXPERT, dtype=jnp.int32)
    table = jnp.sum(jnp.where(named, weights[:, :, None], 0.0), axis=1)
    high = lax.reduce_precision(table, 8, 7)
    low = lax.reduce_precision(table - high, 8, 7)
    extra = jnp.broadcast_to(jnp.concatenate([high, low], axis=1)[:, None, :], (rows, N_DP, PAD - WIDTH))
    tok = jnp.concatenate([tokens.astype(F32).reshape(rows, N_DP, WIDTH), extra], axis=2)
    tok = tok.transpose(1, 0, 2).reshape(N_DP, 2 * rows, 128)
    tok = jnp.pad(tok, ((0, 0), (0, 8 - 2 * rows), (0, 0)))
    dma = pltpu.SemaphoreType.DMA
    vmem = pltpu.VMEM
    half = NZ // 2
    out = pl.pallas_call(
        kernel,
        out_shape=jax.ShapeDtypeStruct((N_DP, 8, 128), F32),
        in_specs=[pl.BlockSpec(memory_space=vmem)] + [pl.BlockSpec(memory_space=pl.ANY)] * 3,
        out_specs=pl.BlockSpec(memory_space=vmem),
        scratch_shapes=[
            vmem((PAD, FFW), BF16),
            vmem((PAD, FFW), BF16),
            vmem((FFW, WIDTH), BF16),
            vmem((N_DP, 8, 128), F32),
            vmem((N_EXPERT, ROWS, PAD), BF16),
            vmem((NZ, NX, CHUNK, 2 * QUARTER), BF16),
            vmem((half, 3, CHUNK, 2 * QUARTER), BF16),
            vmem((half, 7, STRIP, 2 * QUARTER), BF16),
            vmem((half, CHUNK, 2 * QUARTER), BF16),
            vmem((half, 7, NX, STRIP, 2 * QUARTER), BF16),
            vmem((half, NX, STRIP, 2 * QUARTER), BF16),
            vmem((half, 3, STRIP, 2 * QUARTER), BF16),
            vmem((NZ, NX, CHUNK, QUARTER), BF16),
            vmem((NZ, CHUNK, PAD), BF16),
            vmem((2 * NZ, ROWS, PAD), BF16),
            vmem((N_DP, 8, 128), F32),
            vmem((N_DP, 8, 128), F32),
            dma((3,)),
            dma((2,)),
            dma((NZ, 2)),
            dma((NZ, 2)),
            dma((NZ, 10)),
            dma((NZ, 10)),
            dma((NZ, 11)),
            dma((NZ, 11)),
            dma((NZ, 2)),
            dma((NZ, 2)),
            dma((2,)),
        ],
        compiler_params=pltpu.CompilerParams(
            collective_id=0, has_side_effects=True, vmem_limit_bytes=48 * 1024 * 1024
        ),
        name="expert_block",
    )(tok, w_gate, w_up, w_down)
    out = out[:, : 2 * rows].reshape(N_DP, rows, PAD)[:, :, :WIDTH]
    return out.transpose(1, 0, 2).reshape(rows, D).astype(BF16)


def solution(mesh):
    placed = (
        P(("dp", "expert"), None),
        P("expert", "dp", None),
        P("expert", "dp", None),
        P("expert", None, "dp"),
        P(("dp", "expert"), None),
        P(("dp", "expert"), None),
    )
    return jax.shard_map(
        shards, mesh=mesh, in_specs=placed, out_specs=P(("dp", "expert"), None), check_vma=False
    )
```

```python
import jax
import jax.numpy as jnp
from jax import lax
from jax.experimental import pallas as pl
from jax.experimental.pallas import tpu as pltpu
from jax.sharding import PartitionSpec as P

MESH = pl.DeviceIdType.MESH
F32 = jnp.float32
BF16 = jnp.bfloat16

ROUTE_SCALE = 2.5
NX, NY, NZ = 4, 8, 8
N_DP = NX * NY
N_EXPERT = 2 * NZ
D = 7168
WIDTH = D // N_DP
FFW = 1024
PAD = 256
ROWS = 64
CHUNK = 2 * ROWS
UNITS = FFW // NX
STRIP = CHUNK // NY
SHARE = ROWS // NX
OFFSETS = (0, 1, 7, 2, 6, 3, 5, 4)
BACK = tuple(OFFSETS.index((NZ - o) % NZ) for o in OFFSETS)
ARRIVAL = (10.0, 13.6, 13.6, 18.6, 18.6, 23.6, 23.6, 28.6)
STEPS = (1.3, 6.5, 6.0, 6.0)


def kernel(
    tok_ref, wg_hbm, wu_hbm, wd_hbm, out_ref,
    wg, wu, wd, mail, xall, part, rs, hid, outs, xr, so, got, fin_src, fin,
    mail_sem, w_send, w_recv, x_send, x_recv, s_send, s_recv, rs_send, rs_recv, ag_send, ag_recv,
    xr_send, xr_recv, o_send, o_recv, f_send, f_recv,
):
    dp = lax.axis_index("dp")
    e = lax.axis_index("expert")
    X, Y = dp % NX, dp // NX
    Z, C = e // 2, e % 2
    sibling = (dp, Z * 2 + (C + 1) % 2)

    def at(x, y):
        return (lax.rem(y, NY) * NX + lax.rem(x, NX), e)

    barrier = pltpu.get_barrier_semaphore()

    def greet_dp(j, carry):
        pl.semaphore_signal(barrier, inc=1, device_id=((dp + j) % N_DP, e), device_id_type=MESH)
        return carry

    def greet_expert(j, carry):
        pl.semaphore_signal(barrier, inc=1, device_id=(dp, (e + j) % N_EXPERT), device_id_type=MESH)
        return carry

    lax.fori_loop(1, N_DP, greet_dp, 0)
    lax.fori_loop(1, N_EXPERT, greet_expert, 0)

    wg[:, pl.ds(WIDTH, PAD - WIDTH), :] = jnp.zeros((NX, PAD - WIDTH, UNITS), BF16)
    wu[:, pl.ds(WIDTH, PAD - WIDTH), :] = jnp.zeros((NX, PAD - WIDTH, UNITS), BF16)
    outs[...] = jnp.zeros_like(outs)

    pl.semaphore_wait(barrier, N_DP - 1 + N_EXPERT - 1)

    sends = []

    def send(src, dst, send_sem, recv_sem, device):
        copy = pltpu.make_async_remote_copy(src, dst, send_sem, recv_sem, device_id=device, device_id_type=MESH)
        copy.start()
        sends.append(copy)
        return copy

    own_mail = pltpu.make_async_copy(tok_ref.at[Y], mail.at[dp], mail_sem.at[1])
    own_mail.start()

    def post(j, carry):
        d = (dp + j) % N_DP
        pltpu.make_async_remote_copy(
            tok_ref.at[d // NX], mail.at[dp], mail_sem.at[0], mail_sem.at[1],
            device_id=(d, e), device_id_type=MESH,
        ).start()
        return carry

    lax.fori_loop(1, N_DP, post, 0)

    w_copies = []
    for n, (src, dst) in enumerate(((wg_hbm, wg), (wu_hbm, wu), (wd_hbm, wd))):
        for j in (1, 3, 2, 0):
            x = lax.rem(X + j, NX)
            units = pl.ds(pl.multiple_of(x * UNITS, UNITS), UNITS)
            if n < 2:
                a, b = src.at[0, :, units], dst.at[X, pl.ds(0, WIDTH), :]
            else:
                a, b = src.at[0, units, :], dst.at[X]
            if j == 0:
                copy = pltpu.make_async_copy(a, b, w_recv.at[n, 0])
                copy.start()
                w_copies.append((n, copy.wait))
            else:
                copy = send(a, b, w_send.at[n, j], w_recv.at[n, j], at(x, Y))
                w_copies.append((n, copy.wait_recv))

    pltpu.make_async_copy(mail, mail, mail_sem.at[1]).wait()
    size = N_DP * 16
    m = lax.broadcasted_iota(jnp.int32, (size, size), 0)
    n = lax.broadcasted_iota(jnp.int32, (size, size), 1)
    column, turn = (m >> 4) & 3, (m >> 1) & 7
    pick = ((turn * NX + column) * 16 + (m & 1) * 8 + (m >> 6) == n).astype(BF16)
    rows = jnp.dot(pick, mail[...].reshape(size, 128), preferred_element_type=F32).astype(BF16)
    for b in range(NX):
        for h in range(2):
            t = (2 * b + h) * ROWS
            xall[e, b, :, pl.ds(h * 128, 128)] = rows[t:t + ROWS]

    def pass_on(k, block):
        return send(xall.at[block], xall.at[block], s_send.at[k], s_recv.at[k], sibling)

    s_copies, x_copies = {}, {}
    up, down = (dp, (e + 2) % N_EXPERT), (dp, (e + N_EXPERT - 2) % N_EXPERT)

    def forward(k, block, device):
        x_copies[k] = send(xall.at[block], xall.at[block], x_send.at[k], x_recv.at[k], device)

    s_copies[0] = pass_on(0, e)
    forward(OFFSETS.index(1), e, down)
    forward(OFFSETS.index(7), e, up)

    lane = lax.broadcasted_iota(jnp.int32, (CHUNK, PAD), 1)
    mine = (lane == WIDTH + e) | (lane == WIDTH + N_EXPERT + e)
    o_copies = {}

    def ready(n):
        for kind, wait in w_copies:
            if kind == n:
                wait()

    def strip(y):
        return pl.ds(pl.multiple_of(lax.rem(y, NY) * STRIP, STRIP), STRIP)

    def chunk(k):
        off = OFFSETS[k]
        zc = (Z + off) % NZ
        if k > 0:
            block = zc * 2 + C
            x_copies[k].wait_recv()
            if off in (1, 2):
                forward(OFFSETS.index(off + 1), block, down)
            if off in (7, 6, 5):
                forward(OFFSETS.index(off - 1), block, up)
            s_copies[k] = pass_on(k, block)
        yield
        s_copies[k].wait_recv()
        if k == 0:
            ready(0)
            ready(1)

        def block_rows(b):
            return xall[pl.ds(2 * zc, 2), b].reshape(CHUNK, PAD)

        gate = jnp.dot(block_rows(0), wg[0], preferred_element_type=F32)
        up_ = jnp.dot(block_rows(0), wu[0], preferred_element_type=F32)
        for b in range(1, NX):
            gate += jnp.dot(block_rows(b), wg[b], preferred_element_type=F32)
            up_ += jnp.dot(block_rows(b), wu[b], preferred_element_type=F32)
        part[k, :, 0:UNITS] = gate.astype(BF16)
        part[k, :, UNITS:] = up_.astype(BF16)
        copies = []
        for j in (4, 3, 5, 2, 6, 1, 7):
            copies.append(send(
                part.at[k, strip(Y + j)], rs.at[k, j - 1], rs_send.at[k, j - 1], rs_recv.at[k, j - 1], at(X, Y + j)
            ))
        yield
        for copy in copies:
            copy.wait_recv()
        total = part[k, strip(Y)].astype(F32)
        for j in range(NY - 1):
            total += rs[k, j].astype(F32)
        gate, up_ = total[:, :UNITS], total[:, UNITS:]
        hid[k, strip(Y)] = (gate / (1.0 + jnp.exp(-gate)) * up_).astype(BF16)
        piece = hid.at[k, strip(Y)]
        copies = []
        for j in (4, 3, 5, 2, 6, 1, 7):
            copies.append(send(piece, piece, ag_send.at[k, j - 1], ag_recv.at[k, j - 1], at(X, Y + j)))
        yield
        for copy in copies:
            copy.wait_recv()
        if k == 0:
            ready(2)
        weight = jnp.sum(jnp.where(mine, block_rows(0).astype(F32), 0.0), axis=1, keepdims=True)
        for b in range(NX):
            o = jnp.dot(hid[k], wd[b], preferred_element_type=F32) * weight
            o = o.astype(BF16)
            outs[k, 0, b, :, 0:WIDTH] = o[:ROWS]
            outs[k, 1, b, :, 0:WIDTH] = o[ROWS:]

        def share(x):
            return pl.ds(pl.multiple_of(lax.rem(x, NX) * SHARE, SHARE), SHARE)

        copies = []
        for j in (2, 1, 3):
            copies.append(send(
                outs.at[k, :, :, share(X + j)], xr.at[k, j - 1], xr_send.at[k, j - 1], xr_recv.at[k, j - 1],
                at(X + j, Y),
            ))
        yield
        for copy in copies:
            copy.wait_recv()
        total = outs[k, :, :, share(X)].astype(F32)
        for j in range(NX - 1):
            total += xr[k, j].astype(F32)
        so[k] = total.astype(BF16)
        for c in range(2):
            target = (C + c) % 2
            if k == 0 and c == 0:
                got[0] = so[0, C]
                continue
            o_copies[BACK[k], c] = send(
                so.at[k, target], got.at[2 * BACK[k] + c], o_send.at[k, c], o_recv.at[BACK[k], c],
                (dp, zc * 2 + target),
            )

    events = []
    for k in range(NZ):
        when = ARRIVAL[k]
        events.append((when, k))
        for step in STEPS:
            when += step
            events.append((when, k))
    chunks = [chunk(k) for k in range(NZ)]
    for _, k in sorted(events):
        next(chunks[k], None)

    for key in sorted(o_copies):
        o_copies[key].wait_recv()
    total = got[0].astype(F32)
    for t in range(1, 2 * NZ):
        total += got[t].astype(F32)
    total = total.astype(BF16)
    stacked = jnp.concatenate(
        [total[b, :, h * 128:(h + 1) * 128] for b in range(NX) for h in range(2)], axis=0
    )
    m = lax.broadcasted_iota(jnp.int32, (NY * 16, NY * 16), 0)
    n = lax.broadcasted_iota(jnp.int32, (NY * 16, NY * 16), 1)
    place = ((m & 7) * 16 + (m >> 4) * 2 + ((m >> 3) & 1) == n).astype(BF16)
    moved = jnp.dot(place, stacked, preferred_element_type=F32).astype(BF16)
    fin_src[...] = moved.reshape(NY, 16, 128)
    copies = []
    for j in (4, 3, 5, 2, 6, 1, 7):
        y = lax.rem(Y + j, NY)
        copies.append(send(fin_src.at[y], fin.at[Y], f_send.at[j - 1], f_recv.at[j - 1], at(X, y)))
    fin[Y] = fin_src[Y]
    for copy in copies:
        copy.wait_recv()
    out_ref[...] = fin[...]
    pltpu.make_async_copy(mail.at[pl.ds(0, N_DP - 1)], mail.at[pl.ds(0, N_DP - 1)], mail_sem.at[0]).wait()
    for copy in sends:
        copy.wait_send()


def shards(tokens, w_gate, w_up, w_down, routes, scores):
    rows = tokens.shape[0]
    weights = ROUTE_SCALE * scores / jnp.sum(scores, axis=1, keepdims=True)
    named = routes[:, :, None] == jnp.arange(N_EXPERT, dtype=jnp.int32)
    table = jnp.sum(jnp.where(named, weights[:, :, None], 0.0), axis=1)
    high = lax.reduce_precision(table, 8, 7)
    low = lax.reduce_precision(table - high, 8, 7)
    extra = jnp.concatenate([high, low], axis=1).astype(BF16)[:, None, None, :]
    extra = jnp.broadcast_to(extra, (rows, NY, NX, PAD - WIDTH))
    tok = jnp.concatenate([tokens.reshape(rows, NY, NX, WIDTH), extra], axis=3)
    tok = tok.transpose(1, 0, 2, 3).reshape(NY, 16, 128)
    dma = pltpu.SemaphoreType.DMA
    vmem = pltpu.VMEM
    out = pl.pallas_call(
        kernel,
        out_shape=jax.ShapeDtypeStruct((NY, 16, 128), BF16),
        in_specs=[pl.BlockSpec(memory_space=vmem)] + [pl.BlockSpec(memory_space=pl.ANY)] * 3,
        out_specs=pl.BlockSpec(memory_space=vmem),
        scratch_shapes=[
            vmem((NX, PAD, UNITS), BF16),
            vmem((NX, PAD, UNITS), BF16),
            vmem((NX, UNITS, WIDTH), BF16),
            vmem((N_DP, 16, 128), BF16),
            vmem((N_EXPERT, NX, ROWS, PAD), BF16),
            vmem((NZ, CHUNK, 2 * UNITS), BF16),
            vmem((NZ, NY - 1, STRIP, 2 * UNITS), BF16),
            vmem((NZ, CHUNK, UNITS), BF16),
            vmem((NZ, 2, NX, ROWS, PAD), BF16),
            vmem((NZ, NX - 1, 2, NX, SHARE, PAD), BF16),
            vmem((NZ, 2, NX, SHARE, PAD), BF16),
            vmem((2 * NZ, NX, SHARE, PAD), BF16),
            vmem((NY, 16, 128), BF16),
            vmem((NY, 16, 128), BF16),
            dma((2,)),
            dma((3, NX)),
            dma((3, NX)),
            dma((NZ,)),
            dma((NZ,)),
            dma((NZ,)),
            dma((NZ,)),
            dma((NZ, NY - 1)),
            dma((NZ, NY - 1)),
            dma((NZ, NY - 1)),
            dma((NZ, NY - 1)),
            dma((NZ, NX - 1)),
            dma((NZ, NX - 1)),
            dma((NZ, 2)),
            dma((NZ, 2)),
            dma((NY - 1,)),
            dma((NY - 1,)),
        ],
        compiler_params=pltpu.CompilerParams(
            collective_id=0, has_side_effects=True, vmem_limit_bytes=56 * 1024 * 1024
        ),
        name="expert_block",
    )(tok, w_gate, w_up, w_down)
    out = out.reshape(NY, rows, NX, PAD)[:, :, :, :WIDTH]
    return out.transpose(1, 0, 2, 3).reshape(rows, D)


def solution(mesh):
    placed = (
        P(("dp", "expert"), None),
        P("expert", "dp", None),
        P("expert", "dp", None),
        P("expert", None, "dp"),
        P(("dp", "expert"), None),
        P(("dp", "expert"), None),
    )
    return jax.shard_map(
        shards, mesh=mesh, in_specs=placed, out_specs=P(("dp", "expert"), None), check_vma=False
    )
```

```python
import jax
import jax.numpy as jnp
from jax import lax
from jax.experimental import pallas as pl
from jax.experimental.pallas import tpu as pltpu
from jax.sharding import PartitionSpec as P

MESH = pl.DeviceIdType.MESH
F32 = jnp.float32
BF16 = jnp.bfloat16

ROUTE_SCALE = 2.5
NX, NY, NZ = 4, 8, 8
N_DP = NX * NY
N_EXPERT = 2 * NZ
D = 7168
WIDTH = D // N_DP
FFW = 1024
SPAN = NX * WIDTH
GROUPS = SPAN // 128
PAD = SPAN + 128
ROWS = 64
CHUNK = 2 * ROWS
UNITS = FFW // NX
STRIP = CHUNK // NY
SHARE = ROWS // NX
OFFSETS = (0, 1, 7, 2, 6, 3, 5, 4)
BACK = tuple(OFFSETS.index((NZ - o) % NZ) for o in OFFSETS)
ARRIVAL = (10.0, 13.6, 13.6, 18.6, 18.6, 23.6, 23.6, 28.6)
STEPS = (1.3, 6.5, 6.0, 6.0)


def kernel(
    tok_ref, routes_ref, scores_ref, wg_hbm, wu_hbm, wd_hbm, out_ref,
    w_in, w_out, tok_src, mail, xall, part, rs, hid, outs, xr, so, got, fin_src, fin,
    mail_sem, w_send, w_recv, x_send, x_recv, s_send, s_recv, rs_send, rs_recv, ag_send, ag_recv,
    xr_send, xr_recv, o_send, o_recv, f_send, f_recv,
):
    dp = lax.axis_index("dp")
    e = lax.axis_index("expert")
    X, Y = dp % NX, dp // NX
    Z, C = e // 2, e % 2
    sibling = (dp, Z * 2 + (C + 1) % 2)

    def at(x, y):
        return (lax.rem(y, NY) * NX + lax.rem(x, NX), e)

    barrier = pltpu.get_barrier_semaphore()

    def greet_dp(j, carry):
        pl.semaphore_signal(barrier, inc=1, device_id=((dp + j) % N_DP, e), device_id_type=MESH)
        return carry

    def greet_expert(j, carry):
        pl.semaphore_signal(barrier, inc=1, device_id=(dp, (e + j) % N_EXPERT), device_id_type=MESH)
        return carry

    lax.fori_loop(1, N_DP, greet_dp, 0)
    lax.fori_loop(1, N_EXPERT, greet_expert, 0)

    scores = scores_ref[...]
    weights = ROUTE_SCALE * scores / jnp.sum(scores, axis=1, keepdims=True)
    routes = routes_ref[...]
    lanes = lax.broadcasted_iota(jnp.int32, (2, 128), 1)
    table = jnp.zeros((2, 128), F32)
    for k in range(routes.shape[1]):
        table += jnp.where(routes[:, k:k + 1] == (lanes & (N_EXPERT - 1)), weights[:, k:k + 1], 0.0)
    high = table.astype(BF16).astype(F32)
    extra = jnp.where(lanes < N_EXPERT, high, jnp.where(lanes < 2 * N_EXPERT, table - high, 0.0))
    tokens = tok_ref[...].astype(F32)
    for y in range(NY):
        pieces = [tokens[:, y * SPAN + g * 128:y * SPAN + (g + 1) * 128] for g in range(GROUPS)]
        tok_src[y] = jnp.concatenate(pieces + [extra], axis=0).astype(BF16)

    pl.semaphore_wait(barrier, N_DP - 1 + N_EXPERT - 1)

    sends = []

    def send(src, dst, send_sem, recv_sem, device):
        copy = pltpu.make_async_remote_copy(src, dst, send_sem, recv_sem, device_id=device, device_id_type=MESH)
        copy.start()
        sends.append(copy)
        return copy

    own_mail = pltpu.make_async_copy(tok_src.at[Y], mail.at[dp], mail_sem.at[1])
    own_mail.start()

    def post(j, carry):
        d = (dp + j) % N_DP
        pltpu.make_async_remote_copy(
            tok_src.at[d // NX], mail.at[dp], mail_sem.at[0], mail_sem.at[1],
            device_id=(d, e), device_id_type=MESH,
        ).start()
        return carry

    lax.fori_loop(1, N_DP, post, 0)

    w_copies = []
    block = pl.ds(pl.multiple_of(X * WIDTH, 16), WIDTH)
    homes = (w_in.at[block, pl.ds(0, UNITS)], w_in.at[block, pl.ds(UNITS, UNITS)], w_out.at[block])
    for n, (src, b) in enumerate(zip((wg_hbm, wu_hbm, wd_hbm), homes)):
        for j in (1, 3, 2, 0):
            x = lax.rem(X + j, NX)
            a = src.at[0, :, pl.ds(pl.multiple_of(x * UNITS, UNITS), UNITS)]
            if j == 0:
                copy = pltpu.make_async_copy(a, b, w_recv.at[n, 0])
                copy.start()
                w_copies.append((n, copy.wait))
            else:
                copy = send(a, b, w_send.at[n, j], w_recv.at[n, j], at(x, Y))
                w_copies.append((n, copy.wait_recv))

    pltpu.make_async_copy(mail, mail, mail_sem.at[1]).wait()
    size = N_DP * 16
    m = lax.broadcasted_iota(jnp.int32, (size, size), 0)
    n = lax.broadcasted_iota(jnp.int32, (size, size), 1)
    column, turn = (m >> 4) & 3, (m >> 1) & 7
    pick = ((turn * NX + column) * 16 + (m >> 6) * 2 + (m & 1) == n).astype(BF16)
    rows = jnp.dot(pick, mail[...].reshape(size, 128), preferred_element_type=F32).astype(BF16)
    for g in range(GROUPS + 1):
        xall[e, :, pl.ds(g * 128, 128)] = rows[g * ROWS:(g + 1) * ROWS]

    def pass_on(k, block):
        return send(xall.at[block], xall.at[block], s_send.at[k], s_recv.at[k], sibling)

    s_copies, x_copies = {}, {}
    up, down = (dp, (e + 2) % N_EXPERT), (dp, (e + N_EXPERT - 2) % N_EXPERT)

    def forward(k, block, device):
        x_copies[k] = send(xall.at[block], xall.at[block], x_send.at[k], x_recv.at[k], device)

    s_copies[0] = pass_on(0, e)
    forward(OFFSETS.index(1), e, down)
    forward(OFFSETS.index(7), e, up)

    lane = lax.broadcasted_iota(jnp.int32, (CHUNK, 128), 1)
    mine = (lane == e) | (lane == N_EXPERT + e)
    o_copies = {}

    def ready(n):
        for kind, wait in w_copies:
            if kind == n:
                wait()

    def strip(y):
        return pl.ds(pl.multiple_of(lax.rem(y, NY) * STRIP, STRIP), STRIP)

    def chunk(k):
        off = OFFSETS[k]
        zc = (Z + off) % NZ
        if k > 0:
            block = zc * 2 + C
            x_copies[k].wait_recv()
            if off in (1, 2):
                forward(OFFSETS.index(off + 1), block, down)
            if off in (7, 6, 5):
                forward(OFFSETS.index(off - 1), block, up)
            s_copies[k] = pass_on(k, block)
        yield
        s_copies[k].wait_recv()
        if k == 0:
            ready(0)
            ready(1)

        x = xall[pl.ds(2 * zc, 2), :, 0:SPAN].reshape(CHUNK, SPAN)
        part[k] = jnp.dot(x, w_in[...], preferred_element_type=F32).astype(BF16)
        copies = []
        for j in (4, 3, 5, 2, 6, 1, 7):
            copies.append(send(
                part.at[k, strip(Y + j)], rs.at[k, j - 1], rs_send.at[k, j - 1], rs_recv.at[k, j - 1], at(X, Y + j)
            ))
        yield
        for copy in copies:
            copy.wait_recv()
        total = part[k, strip(Y)].astype(F32)
        for j in range(NY - 1):
            total += rs[k, j].astype(F32)
        gate, up_ = total[:, :UNITS], total[:, UNITS:]
        hid[k, strip(Y)] = (gate / (1.0 + jnp.exp(-gate)) * up_).astype(BF16)
        piece = hid.at[k, strip(Y)]
        copies = []
        for j in (4, 3, 5, 2, 6, 1, 7):
            copies.append(send(piece, piece, ag_send.at[k, j - 1], ag_recv.at[k, j - 1], at(X, Y + j)))
        yield
        for copy in copies:
            copy.wait_recv()
        if k == 0:
            ready(2)
        extra = xall[pl.ds(2 * zc, 2), :, SPAN:].reshape(CHUNK, 128).astype(F32)
        weight = jnp.sum(jnp.where(mine, extra, 0.0), axis=1, keepdims=True)
        o = lax.dot_general(hid[k], w_out[...], (((1,), (1,)), ((), ())), preferred_element_type=F32)
        outs[k] = (o * weight).astype(BF16).reshape(2, ROWS, SPAN)

        def share(x):
            return pl.ds(pl.multiple_of(lax.rem(x, NX) * SHARE, SHARE), SHARE)

        copies = []
        for j in (2, 1, 3):
            copies.append(send(
                outs.at[k, :, share(X + j)], xr.at[k, j - 1], xr_send.at[k, j - 1], xr_recv.at[k, j - 1],
                at(X + j, Y),
            ))
        yield
        for copy in copies:
            copy.wait_recv()
        total = outs[k, :, share(X)].astype(F32)
        for j in range(NX - 1):
            total += xr[k, j].astype(F32)
        so[k] = total.astype(BF16)
        for c in range(2):
            target = (C + c) % 2
            if k == 0 and c == 0:
                got[0] = so[0, C]
                continue
            o_copies[BACK[k], c] = send(
                so.at[k, target], got.at[2 * BACK[k] + c], o_send.at[k, c], o_recv.at[BACK[k], c],
                (dp, zc * 2 + target),
            )

    events = []
    for k in range(NZ):
        when = ARRIVAL[k]
        events.append((when, k))
        for step in STEPS:
            when += step
            events.append((when, k))
    chunks = [chunk(k) for k in range(NZ)]
    for _, k in sorted(events):
        next(chunks[k], None)

    for key in sorted(o_copies):
        o_copies[key].wait_recv()
    total = got[0].astype(F32)
    for t in range(1, 2 * NZ):
        total += got[t].astype(F32)
    total = total.astype(BF16)
    stacked = jnp.concatenate([total[:, g * 128:(g + 1) * 128] for g in range(GROUPS)], axis=0)
    m = lax.broadcasted_iota(jnp.int32, (NY * 16, GROUPS * 16), 0)
    n = lax.broadcasted_iota(jnp.int32, (NY * 16, GROUPS * 16), 1)
    place = (((m >> 1) & 7) * 16 + (m >> 4) * 2 + (m & 1) == n).astype(BF16)
    moved = jnp.dot(place, stacked, preferred_element_type=F32).astype(BF16)
    fin_src[...] = moved.reshape(NY, 16, 128)
    copies = []
    for j in (4, 3, 5, 2, 6, 1, 7):
        y = lax.rem(Y + j, NY)
        copies.append(send(fin_src.at[y], fin.at[Y], f_send.at[j - 1], f_recv.at[j - 1], at(X, y)))
    fin[Y] = fin_src[Y]
    for copy in copies:
        copy.wait_recv()
    pieces = []
    for y in range(NY):
        tile = fin[y].astype(F32)
        pieces += [tile[2 * g:2 * g + 2] for g in range(GROUPS)]
    out_ref[...] = jnp.concatenate(pieces, axis=1).astype(BF16)
    pltpu.make_async_copy(mail.at[pl.ds(0, N_DP - 1)], mail.at[pl.ds(0, N_DP - 1)], mail_sem.at[0]).wait()
    for copy in sends:
        copy.wait_send()


def shards(tokens, w_gate, w_up, w_down, routes, scores):
    dma = pltpu.SemaphoreType.DMA
    vmem = pltpu.VMEM
    return pl.pallas_call(
        kernel,
        out_shape=jax.ShapeDtypeStruct(tokens.shape, BF16),
        in_specs=[pl.BlockSpec(memory_space=vmem)] * 3 + [pl.BlockSpec(memory_space=pl.ANY)] * 3,
        out_specs=pl.BlockSpec(memory_space=vmem),
        scratch_shapes=[
            vmem((SPAN, 2 * UNITS), BF16),
            vmem((SPAN, UNITS), BF16),
            vmem((NY, 16, 128), BF16),
            vmem((N_DP, 16, 128), BF16),
            vmem((N_EXPERT, ROWS, PAD), BF16),
            vmem((NZ, CHUNK, 2 * UNITS), BF16),
            vmem((NZ, NY - 1, STRIP, 2 * UNITS), BF16),
            vmem((NZ, CHUNK, UNITS), BF16),
            vmem((NZ, 2, ROWS, SPAN), BF16),
            vmem((NZ, NX - 1, 2, SHARE, SPAN), BF16),
            vmem((NZ, 2, SHARE, SPAN), BF16),
            vmem((2 * NZ, SHARE, SPAN), BF16),
            vmem((NY, 16, 128), BF16),
            vmem((NY, 16, 128), BF16),
            dma((2,)),
            dma((3, NX)),
            dma((3, NX)),
            dma((NZ,)),
            dma((NZ,)),
            dma((NZ,)),
            dma((NZ,)),
            dma((NZ, NY - 1)),
            dma((NZ, NY - 1)),
            dma((NZ, NY - 1)),
            dma((NZ, NY - 1)),
            dma((NZ, NX - 1)),
            dma((NZ, NX - 1)),
            dma((NZ, 2)),
            dma((NZ, 2)),
            dma((NY - 1,)),
            dma((NY - 1,)),
        ],
        compiler_params=pltpu.CompilerParams(
            collective_id=0, has_side_effects=True, vmem_limit_bytes=56 * 1024 * 1024
        ),
        name="expert_block",
    )(tokens, routes, scores, w_gate, w_up, w_down.swapaxes(1, 2))


def solution(mesh):
    placed = (
        P(("dp", "expert"), None),
        P("expert", "dp", None),
        P("expert", "dp", None),
        P("expert", None, "dp"),
        P(("dp", "expert"), None),
        P(("dp", "expert"), None),
    )
    return jax.shard_map(
        shards, mesh=mesh, in_specs=placed, out_specs=P(("dp", "expert"), None), check_vma=False
    )
```

```python
import jax
import jax.numpy as jnp
from jax import lax
from jax.experimental import pallas as pl
from jax.experimental.pallas import tpu as pltpu
from jax.sharding import PartitionSpec as P

MESH = pl.DeviceIdType.MESH
F32 = jnp.float32
BF16 = jnp.bfloat16

ROUTE_SCALE = 2.5
NX, NY, NZ = 4, 8, 8
N_DP = NX * NY
N_EXPERT = 2 * NZ
D = 7168
WIDTH = D // N_DP
FFW = 1024
SPAN = NX * WIDTH
GROUPS = SPAN // 128
PAD = SPAN + 128
ROWS = 64
CHUNK = 2 * ROWS
UNITS = FFW // NX
STRIP = CHUNK // NY
SHARE = ROWS // NX
OFFSETS = (0, 1, 7, 2, 6, 3, 5, 4)
BACK = tuple(OFFSETS.index((NZ - o) % NZ) for o in OFFSETS)
STRAIGHT = ()
FAR_FIRST = (4, 3, 5, 2, 6, 1, 7)
FROM_Z = (9.3, 13.3, 13.8, 15.3, 15.8, 17.3, 17.8, 18.8)
FROM_X = (15, 17.5, 18.5, 20, 21, 22, 23, 24)
START = (16.6, 18.9, 19.9, 21.4, 22.6, 24.1, 25.6, 27.1)
HOP = 4.5


def plan():
    events = []
    for k in range(NZ):
        times = [FROM_Z[k], FROM_X[k], START[k]]
        waits = (1.5 * HOP, 1.3 * HOP) if k in STRAIGHT else (HOP,) * 4
        for wait in waits + (1.6, HOP):
            times.append(times[-1] + wait)
        events += [(when, k) for when in times]
    return [k for _, k in sorted(events)]


def kernel(
    tok_ref, routes_ref, scores_ref, wg_hbm, wu_hbm, wd_hbm, out_ref,
    w_in, w_out, tok_src, mail, xall, part, rs, hid, outs, core, so, xr, zs, got, fin_src, fin,
    m_send, m_recv, w_send, w_recv, z_send, z_recv, x_send, x_recv, s_send, s_recv, rs_send, rs_recv, ag_send, ag_recv,
    c_send, c_recv, xr_send, xr_recv, o_send, o_recv, f_send, f_recv,
):
    dp = lax.axis_index("dp")
    e = lax.axis_index("expert")
    X, Y = dp % NX, dp // NX
    Z, C = e // 2, e % 2
    sibling = (dp, Z * 2 + (C + 1) % 2)

    def at(x, y):
        return (lax.rem(y, NY) * NX + lax.rem(x, NX), e)

    barrier = pltpu.get_barrier_semaphore()

    peers = [at(X, Y + j) for j in range(1, NY)] + [sibling]
    peers += [at(X + j, Y) for j in range(1, NX)] + [(dp, lax.rem(e + 2 * j, N_EXPERT)) for j in range(1, NZ)]
    for peer in peers:
        pl.semaphore_signal(barrier, inc=1, device_id=peer, device_id_type=MESH)

    pl.semaphore_wait(barrier, len(peers))

    sends = []

    def send(src, dst, send_sem, recv_sem, device):
        copy = pltpu.make_async_remote_copy(src, dst, send_sem, recv_sem, device_id=device, device_id_type=MESH)
        copy.start()
        sends.append(copy)
        return copy

    w_copies = []
    block = pl.ds(pl.multiple_of(X * WIDTH, 16), WIDTH)
    homes = (w_in.at[block, pl.ds(0, UNITS)], w_in.at[block, pl.ds(UNITS, UNITS)], w_out.at[block])

    def give(n, src, b):
        for j in (2, 1, 3, 0):
            x = lax.rem(X + j, NX)
            a = src.at[0, :, pl.ds(pl.multiple_of(x * UNITS, UNITS), UNITS)]
            if j == 0:
                copy = pltpu.make_async_copy(a, b, w_recv.at[n, 0])
                copy.start()
                w_copies.append((n, copy.wait))
            else:
                copy = send(a, b, w_send.at[n, j], w_recv.at[n, j], at(x, Y))
                w_copies.append((n, copy.wait_recv))

    give(0, wg_hbm, homes[0])
    give(1, wu_hbm, homes[1])

    scores = scores_ref[...]
    weights = ROUTE_SCALE * scores / jnp.sum(scores, axis=1, keepdims=True)
    routes = routes_ref[...]
    lanes = lax.broadcasted_iota(jnp.int32, (2, 128), 1)
    table = jnp.zeros((2, 128), F32)
    for k in range(routes.shape[1]):
        table += jnp.where(routes[:, k:k + 1] == (lanes & (N_EXPERT - 1)), weights[:, k:k + 1], 0.0)
    high = table.astype(BF16).astype(F32)
    extra = jnp.where(lanes < N_EXPERT, high, jnp.where(lanes < 2 * N_EXPERT, table - high, 0.0))
    tokens = tok_ref[...].astype(F32)
    for y in range(NY):
        pieces = [tokens[:, y * SPAN + g * 128:y * SPAN + (g + 1) * 128] for g in range(GROUPS)]
        tok_src[y] = jnp.concatenate(pieces + [extra], axis=0).astype(BF16)

    mail_copies = []
    for j in FAR_FIRST:
        y = lax.rem(Y + j, NY)
        mail_copies.append(send(tok_src.at[y], mail.at[Y], m_send.at[j - 1], m_recv.at[j - 1], at(X, y)))
    mail[Y] = tok_src[Y]

    for copy in mail_copies:
        copy.wait_recv()
    size = NY * 16
    m = lax.broadcasted_iota(jnp.int32, (size, size), 0)
    n = lax.broadcasted_iota(jnp.int32, (size, size), 1)
    pick = (((m >> 1) & 7) * 16 + (m >> 4) * 2 + (m & 1) == n).astype(BF16)
    rows = jnp.dot(pick, mail[...].reshape(size, 128), preferred_element_type=F32).astype(BF16)

    def share(x):
        return pl.ds(pl.multiple_of(lax.rem(x, NX) * SHARE, SHARE), SHARE)

    for g in range(GROUPS + 1):
        xall[e, share(X), pl.ds(g * 128, 128)] = rows[g * SHARE:(g + 1) * SHARE]

    own = xall.at[e, share(X)]
    z_copies = {}
    for k in range(1, NZ):
        there = (dp, lax.rem(e + 2 * OFFSETS[k], N_EXPERT))
        z_copies[BACK[k]] = send(own, own, z_send.at[k], z_recv.at[BACK[k]], there)

    lane = lax.broadcasted_iota(jnp.int32, (CHUNK, 128), 1)
    mine = (lane == e) | (lane == N_EXPERT + e)
    o_copies = {}

    def ready(n):
        for kind, wait in w_copies:
            if kind == n:
                wait()

    def strip(y):
        return pl.ds(pl.multiple_of(lax.rem(y, NY) * STRIP, STRIP), STRIP)

    def sum_send(k, n, src, j):
        return send(src, rs.at[k, n], rs_send.at[k, n], rs_recv.at[k, n], at(X, Y + j + NY))

    def sum_straight(k):
        copies = [sum_send(k, j - 1, part.at[k, strip(Y + j)], j) for j in FAR_FIRST]
        yield
        for copy in copies:
            copy.wait_recv()

    def sum_tree(k, t):
        def piece(j):
            return part.at[k, strip(Y + j + NY)]

        a = sum_send(k, 0, piece(4), 2 * t)
        b = sum_send(k, 1, piece(3 * t), t)
        c = sum_send(k, 2, piece(-3 * t), -t)
        last = [sum_send(k, 3, piece(t), t), sum_send(k, 4, piece(-t), -t)]
        yield
        c.wait_recv()
        rs[k, 2] = (rs[k, 2].astype(F32) + piece(-2 * t)[...].astype(F32)).astype(BF16)
        last.append(sum_send(k, 5, rs.at[k, 2], -2 * t))
        a.wait_recv()
        b.wait_recv()
        total = rs[k, 0].astype(F32) + rs[k, 1].astype(F32) + piece(2 * t)[...].astype(F32)
        rs[k, 0] = total.astype(BF16)
        last.append(sum_send(k, 6, rs.at[k, 0], 2 * t))
        yield
        for copy in last:
            copy.wait_recv()

    def gather_send(k, n, source, j):
        ref = hid.at[k, strip(Y + source + NY)]
        return send(ref, ref, ag_send.at[k, n], ag_recv.at[k, n], at(X, Y + j + NY))

    def gather_straight(k):
        copies = [gather_send(k, j - 1, 0, j) for j in FAR_FIRST]
        yield
        for copy in copies:
            copy.wait_recv()

    def gather_tree(k, t):
        a = gather_send(k, 0, 0, 2 * t)
        b = gather_send(k, 1, 0, -2 * t)
        last = [gather_send(k, 2, 0, t), gather_send(k, 3, 0, -t)]
        yield
        a.wait_recv()
        last.append(gather_send(k, 4, -2 * t, 2 * t))
        last.append(gather_send(k, 5, -2 * t, t))
        b.wait_recv()
        last.append(gather_send(k, 6, 2 * t, -t))
        yield
        for copy in last:
            copy.wait_recv()

    def chunk(k):
        off = OFFSETS[k]
        zc = (Z + off) % NZ
        block = zc * 2 + C
        if k > 0:
            z_copies[k].wait_recv()
        rows = xall.at[block, share(X)]
        copies = []
        for j in (2, 1, 3):
            copies.append(send(rows, rows, x_send.at[k, j - 1], x_recv.at[k, j - 1], at(X + j, Y)))
        if k == NZ - 1:
            give(2, wd_hbm, homes[2])
        yield
        for copy in copies:
            copy.wait_recv()
        copy = send(xall.at[block], xall.at[block], s_send.at[k], s_recv.at[k], sibling)
        yield
        copy.wait_recv()
        if k == 0:
            ready(0)
            ready(1)
        x = xall[pl.ds(2 * zc, 2), :, 0:SPAN].reshape(CHUNK, SPAN)
        part[k] = jnp.dot(x, w_in[...], preferred_element_type=F32).astype(BF16)
        turn = 1 if k % 2 == 0 else -1
        if k in STRAIGHT:
            yield from sum_straight(k)
            parts = [rs[k, j] for j in range(NY - 1)]
        else:
            yield from sum_tree(k, turn)
            parts = [rs[k, j] for j in (3, 4, 5, 6)]
        total = part[k, strip(Y)].astype(F32)
        for value in parts:
            total += value.astype(F32)
        gate, up_ = total[:, :UNITS], total[:, UNITS:]
        hid[k, strip(Y)] = (gate / (1.0 + jnp.exp(-gate)) * up_).astype(BF16)
        if k in STRAIGHT:
            yield from gather_straight(k)
        else:
            yield from gather_tree(k, turn)
        if k == 0:
            ready(2)
        extra = xall[pl.ds(2 * zc, 2), :, SPAN:].reshape(CHUNK, 128).astype(F32)
        weight = jnp.sum(jnp.where(mine, extra, 0.0), axis=1, keepdims=True)
        o = lax.dot_general(hid[k], w_out[...], (((1,), (1,)), ((), ())), preferred_element_type=F32)
        outs[k] = (o * weight).astype(BF16).reshape(2, ROWS, SPAN)
        copy = send(outs.at[k, lax.rem(C + 1, 2)], core.at[k], c_send.at[k], c_recv.at[k], sibling)
        yield
        copy.wait_recv()
        so[k] = (outs[k, C].astype(F32) + core[k].astype(F32)).astype(BF16)
        copies = []
        for j in (2, 1, 3):
            copies.append(send(
                so.at[k, share(X + j)], xr.at[k, j - 1], xr_send.at[k, j - 1], xr_recv.at[k, j - 1], at(X + j, Y)
            ))
        yield
        for copy in copies:
            copy.wait_recv()
        total = so[k, share(X)].astype(F32)
        for j in range(NX - 1):
            total += xr[k, j].astype(F32)
        if k == 0:
            got[0] = total.astype(BF16)
            return
        zs[k] = total.astype(BF16)
        o_copies[BACK[k]] = send(
            zs.at[k], got.at[BACK[k]], o_send.at[k], o_recv.at[BACK[k]], (dp, lax.rem(e + 2 * off, N_EXPERT))
        )

    chunks = [chunk(k) for k in range(NZ)]
    for k in plan():
        next(chunks[k], None)

    for key in sorted(o_copies):
        o_copies[key].wait_recv()
    total = jnp.zeros((SHARE, SPAN), F32)
    for k in range(NZ):
        total += got[k].astype(F32)
    total = total.astype(BF16)
    stacked = jnp.concatenate([total[:, g * 128:(g + 1) * 128] for g in range(GROUPS)], axis=0)
    m = lax.broadcasted_iota(jnp.int32, (NY * 16, GROUPS * 16), 0)
    n = lax.broadcasted_iota(jnp.int32, (NY * 16, GROUPS * 16), 1)
    place = (((m >> 1) & 7) * 16 + (m >> 4) * 2 + (m & 1) == n).astype(BF16)
    moved = jnp.dot(place, stacked, preferred_element_type=F32).astype(BF16)
    fin_src[...] = moved.reshape(NY, 16, 128)
    copies = []
    for j in FAR_FIRST:
        y = lax.rem(Y + j, NY)
        copies.append(send(fin_src.at[y], fin.at[Y], f_send.at[j - 1], f_recv.at[j - 1], at(X, y)))
    fin[Y] = fin_src[Y]
    for copy in copies:
        copy.wait_recv()
    pieces = []
    for y in range(NY):
        tile = fin[y].astype(F32)
        pieces += [tile[2 * g:2 * g + 2] for g in range(GROUPS)]
    out_ref[...] = jnp.concatenate(pieces, axis=1).astype(BF16)
    for copy in sends:
        copy.wait_send()


def shards(tokens, w_gate, w_up, w_down, routes, scores):
    dma = pltpu.SemaphoreType.DMA
    vmem = pltpu.VMEM
    return pl.pallas_call(
        kernel,
        out_shape=jax.ShapeDtypeStruct(tokens.shape, BF16),
        in_specs=[pl.BlockSpec(memory_space=vmem)] * 3 + [pl.BlockSpec(memory_space=pl.ANY)] * 3,
        out_specs=pl.BlockSpec(memory_space=vmem),
        scratch_shapes=[
            vmem((SPAN, 2 * UNITS), BF16),
            vmem((SPAN, UNITS), BF16),
            vmem((NY, 16, 128), BF16),
            vmem((NY, 16, 128), BF16),
            vmem((N_EXPERT, ROWS, PAD), BF16),
            vmem((NZ, CHUNK, 2 * UNITS), BF16),
            vmem((NZ, NY - 1, STRIP, 2 * UNITS), BF16),
            vmem((NZ, CHUNK, UNITS), BF16),
            vmem((NZ, 2, ROWS, SPAN), BF16),
            vmem((NZ, ROWS, SPAN), BF16),
            vmem((NZ, ROWS, SPAN), BF16),
            vmem((NZ, NX - 1, SHARE, SPAN), BF16),
            vmem((NZ, SHARE, SPAN), BF16),
            vmem((NZ, SHARE, SPAN), BF16),
            vmem((NY, 16, 128), BF16),
            vmem((NY, 16, 128), BF16),
            dma((NY - 1,)),
            dma((NY - 1,)),
            dma((3, NX)),
            dma((3, NX)),
            dma((NZ,)),
            dma((NZ,)),
            dma((NZ, NX - 1)),
            dma((NZ, NX - 1)),
            dma((NZ,)),
            dma((NZ,)),
            dma((NZ, NY - 1)),
            dma((NZ, NY - 1)),
            dma((NZ, NY - 1)),
            dma((NZ, NY - 1)),
            dma((NZ,)),
            dma((NZ,)),
            dma((NZ, NX - 1)),
            dma((NZ, NX - 1)),
            dma((NZ,)),
            dma((NZ,)),
            dma((NY - 1,)),
            dma((NY - 1,)),
        ],
        compiler_params=pltpu.CompilerParams(
            collective_id=0, has_side_effects=True, vmem_limit_bytes=56 * 1024 * 1024
        ),
        name="expert_block",
    )(tokens, routes, scores, w_gate, w_up, w_down.swapaxes(1, 2))


def solution(mesh):
    placed = (
        P(("dp", "expert"), None),
        P("expert", "dp", None),
        P("expert", "dp", None),
        P("expert", None, "dp"),
        P(("dp", "expert"), None),
        P(("dp", "expert"), None),
    )
    return jax.shard_map(
        shards, mesh=mesh, in_specs=placed, out_specs=P(("dp", "expert"), None), check_vma=False
    )
```

```python
import jax
import jax.numpy as jnp
from jax import lax
from jax.experimental import pallas as pl
from jax.experimental.pallas import tpu as pltpu
from jax.sharding import PartitionSpec as P

MESH = pl.DeviceIdType.MESH
F32 = jnp.float32
BF16 = jnp.bfloat16

ROUTE_SCALE = 2.5
NX, NY, NZ = 4, 8, 8
N_DP = NX * NY
N_EXPERT = 2 * NZ
D = 7168
WIDTH = D // N_DP
FFW = 1024
SPAN = NX * WIDTH
GROUPS = SPAN // 128
PAD = SPAN + 128
ROWS = 64
CHUNK = 2 * ROWS
UNITS = FFW // NX
STRIP = CHUNK // NY
SHARE = ROWS // NX
OFFSETS = (0, 1, 4, 3, 5, 2, 6, 7)
BACK = tuple(OFFSETS.index((NZ - o) % NZ) for o in OFFSETS)
STRAIGHT = ()
FAR_FIRST = (4, 3, 5, 2, 6, 1, 7)
FROM_Z = (9.3, 13.3, 15.8, 16.6, 16.9, 17.4, 17.7, 18.0)
FROM_X = (15, 17.5, 20, 21, 21.8, 22.8, 23.8, 24.8)
START = (16.6, 18.9, 21.4, 22.4, 23.2, 24.2, 25.6, 27.1)
HOP = 3.8


def plan():
    events = []
    for k in range(NZ):
        times = [FROM_Z[k], FROM_X[k], START[k]]
        waits = (1.5 * HOP, 1.3 * HOP) if k in STRAIGHT else (HOP,) * 4
        for wait in waits + (1.6, HOP):
            times.append(times[-1] + wait)
        events += [(when, k) for when in times]
    return [k for _, k in sorted(events)]


def kernel(
    tok_hbm, routes_hbm, scores_hbm, wg_hbm, wu_hbm, wd_hbm, out_ref,
    tok_ref, routes_ref, scores_ref, w_in, w_out, tok_src, mail, xall, part, rs, hid, outs, core, so, xr, zs, got, fin_src, fin,
    in_sem, m_send, m_recv, w_send, w_recv, z_send, z_recv, x_send, x_recv, s_send, s_recv, rs_send, rs_recv, ag_send, ag_recv,
    c_send, c_recv, xr_send, xr_recv, o_send, o_recv, f_send, f_recv,
):
    dp = lax.axis_index("dp")
    e = lax.axis_index("expert")
    X, Y = dp % NX, dp // NX
    Z, C = e // 2, e % 2
    sibling = (dp, Z * 2 + (C + 1) % 2)

    def at(x, y):
        return (lax.rem(y, NY) * NX + lax.rem(x, NX), e)

    loads = [
        pltpu.make_async_copy(src, dst, in_sem.at[n])
        for n, (src, dst) in enumerate(((tok_hbm, tok_ref), (routes_hbm, routes_ref), (scores_hbm, scores_ref)))
    ]
    for load in loads:
        load.start()

    barrier = pltpu.get_barrier_semaphore()

    peers = [at(X, Y + j) for j in range(1, NY)] + [sibling]
    peers += [at(X + j, Y) for j in range(1, NX)] + [(dp, lax.rem(e + 2 * j, N_EXPERT)) for j in range(1, NZ)]
    for peer in peers:
        pl.semaphore_signal(barrier, inc=1, device_id=peer, device_id_type=MESH)

    pl.semaphore_wait(barrier, len(peers))

    sends = []

    def send(src, dst, send_sem, recv_sem, device):
        copy = pltpu.make_async_remote_copy(src, dst, send_sem, recv_sem, device_id=device, device_id_type=MESH)
        copy.start()
        sends.append(copy)
        return copy

    w_copies = []
    block = pl.ds(pl.multiple_of(X * WIDTH, 16), WIDTH)
    homes = (w_in.at[block, pl.ds(0, UNITS)], w_in.at[block, pl.ds(UNITS, UNITS)], w_out.at[block])

    def give(n, src, b):
        for j in (2, 1, 3, 0):
            x = lax.rem(X + j, NX)
            a = src.at[0, :, pl.ds(pl.multiple_of(x * UNITS, UNITS), UNITS)]
            if j == 0:
                copy = pltpu.make_async_copy(a, b, w_recv.at[n, 0])
                copy.start()
                w_copies.append((n, copy.wait))
            else:
                copy = send(a, b, w_send.at[n, j], w_recv.at[n, j], at(x, Y))
                w_copies.append((n, copy.wait_recv))

    give(0, wg_hbm, homes[0])
    give(1, wu_hbm, homes[1])

    for load in loads:
        load.wait()
    scores = scores_ref[...]
    weights = ROUTE_SCALE * scores / jnp.sum(scores, axis=1, keepdims=True)
    routes = routes_ref[...]
    lanes = lax.broadcasted_iota(jnp.int32, (2, 128), 1)
    table = jnp.zeros((2, 128), F32)
    for k in range(routes.shape[1]):
        table += jnp.where(routes[:, k:k + 1] == (lanes & (N_EXPERT - 1)), weights[:, k:k + 1], 0.0)
    high = table.astype(BF16).astype(F32)
    extra = jnp.where(lanes < N_EXPERT, high, jnp.where(lanes < 2 * N_EXPERT, table - high, 0.0))
    tokens = tok_ref[...].astype(F32)
    for y in range(NY):
        pieces = [tokens[:, y * SPAN + g * 128:y * SPAN + (g + 1) * 128] for g in range(GROUPS)]
        tok_src[y] = jnp.concatenate(pieces + [extra], axis=0).astype(BF16)

    mail_copies = []
    for j in FAR_FIRST:
        y = lax.rem(Y + j, NY)
        mail_copies.append(send(tok_src.at[y], mail.at[Y], m_send.at[j - 1], m_recv.at[j - 1], at(X, y)))
    mail[Y] = tok_src[Y]

    for copy in mail_copies:
        copy.wait_recv()
    size = NY * 16
    m = lax.broadcasted_iota(jnp.int32, (size, size), 0)
    n = lax.broadcasted_iota(jnp.int32, (size, size), 1)
    pick = (((m >> 1) & 7) * 16 + (m >> 4) * 2 + (m & 1) == n).astype(BF16)
    rows = jnp.dot(pick, mail[...].reshape(size, 128), preferred_element_type=F32).astype(BF16)

    def share(x):
        return pl.ds(pl.multiple_of(lax.rem(x, NX) * SHARE, SHARE), SHARE)

    for g in range(GROUPS + 1):
        xall[e, share(X), pl.ds(g * 128, 128)] = rows[g * SHARE:(g + 1) * SHARE]

    own = xall.at[e, share(X)]
    z_copies = {}
    for k in range(1, NZ):
        there = (dp, lax.rem(e + 2 * OFFSETS[k], N_EXPERT))
        z_copies[BACK[k]] = send(own, own, z_send.at[k], z_recv.at[BACK[k]], there)

    lane = lax.broadcasted_iota(jnp.int32, (CHUNK, 128), 1)
    mine = (lane == e) | (lane == N_EXPERT + e)
    o_copies = {}

    def ready(n):
        for kind, wait in w_copies:
            if kind == n:
                wait()

    def strip(y):
        return pl.ds(pl.multiple_of(lax.rem(y, NY) * STRIP, STRIP), STRIP)

    def sum_send(k, n, src, j):
        return send(src, rs.at[k, n], rs_send.at[k, n], rs_recv.at[k, n], at(X, Y + j + NY))

    def sum_straight(k):
        copies = [sum_send(k, j - 1, part.at[k, strip(Y + j)], j) for j in FAR_FIRST]
        yield
        for copy in copies:
            copy.wait_recv()

    def sum_tree(k, t):
        def piece(j):
            return part.at[k, strip(Y + j + NY)]

        a = sum_send(k, 0, piece(4), 2 * t)
        b = sum_send(k, 1, piece(3 * t), t)
        c = sum_send(k, 2, piece(-3 * t), -t)
        last = [sum_send(k, 3, piece(t), t), sum_send(k, 4, piece(-t), -t)]
        yield
        c.wait_recv()
        rs[k, 2] = (rs[k, 2].astype(F32) + piece(-2 * t)[...].astype(F32)).astype(BF16)
        last.append(sum_send(k, 5, rs.at[k, 2], -2 * t))
        a.wait_recv()
        b.wait_recv()
        total = rs[k, 0].astype(F32) + rs[k, 1].astype(F32) + piece(2 * t)[...].astype(F32)
        rs[k, 0] = total.astype(BF16)
        last.append(sum_send(k, 6, rs.at[k, 0], 2 * t))
        yield
        for copy in last:
            copy.wait_recv()

    def gather_send(k, n, source, j):
        ref = hid.at[k, strip(Y + source + NY)]
        return send(ref, ref, ag_send.at[k, n], ag_recv.at[k, n], at(X, Y + j + NY))

    def gather_straight(k):
        copies = [gather_send(k, j - 1, 0, j) for j in FAR_FIRST]
        yield
        for copy in copies:
            copy.wait_recv()

    def gather_tree(k, t):
        a = gather_send(k, 0, 0, 2 * t)
        b = gather_send(k, 1, 0, -2 * t)
        last = [gather_send(k, 2, 0, t), gather_send(k, 3, 0, -t)]
        yield
        a.wait_recv()
        last.append(gather_send(k, 4, -2 * t, 2 * t))
        last.append(gather_send(k, 5, -2 * t, t))
        b.wait_recv()
        last.append(gather_send(k, 6, 2 * t, -t))
        yield
        for copy in last:
            copy.wait_recv()

    def chunk(k):
        off = OFFSETS[k]
        zc = (Z + off) % NZ
        block = zc * 2 + C
        if k > 0:
            z_copies[k].wait_recv()
        rows = xall.at[block, share(X)]
        copies = []
        for j in (2, 1, 3):
            copies.append(send(rows, rows, x_send.at[k, j - 1], x_recv.at[k, j - 1], at(X + j, Y)))
        if k == NZ - 1:
            give(2, wd_hbm, homes[2])
        yield
        for copy in copies:
            copy.wait_recv()
        copy = send(xall.at[block], xall.at[block], s_send.at[k], s_recv.at[k], sibling)
        yield
        copy.wait_recv()
        if k == 0:
            ready(0)
            ready(1)
        x = xall[pl.ds(2 * zc, 2), :, 0:SPAN].reshape(CHUNK, SPAN)
        part[k] = jnp.dot(x, w_in[...], preferred_element_type=F32).astype(BF16)
        turn = 1 if k % 2 == 0 else -1
        if k in STRAIGHT:
            yield from sum_straight(k)
            parts = [rs[k, j] for j in range(NY - 1)]
        else:
            yield from sum_tree(k, turn)
            parts = [rs[k, j] for j in (3, 4, 5, 6)]
        total = part[k, strip(Y)].astype(F32)
        for value in parts:
            total += value.astype(F32)
        gate, up_ = total[:, :UNITS], total[:, UNITS:]
        hid[k, strip(Y)] = (gate / (1.0 + jnp.exp(-gate)) * up_).astype(BF16)
        if k in STRAIGHT:
            yield from gather_straight(k)
        else:
            yield from gather_tree(k, turn)
        if k == 0:
            ready(2)
        extra = xall[pl.ds(2 * zc, 2), :, SPAN:].reshape(CHUNK, 128).astype(F32)
        weight = jnp.sum(jnp.where(mine, extra, 0.0), axis=1, keepdims=True)
        o = lax.dot_general(hid[k], w_out[...], (((1,), (1,)), ((), ())), preferred_element_type=F32)
        outs[k] = (o * weight).astype(BF16).reshape(2, ROWS, SPAN)
        copy = send(outs.at[k, lax.rem(C + 1, 2)], core.at[k], c_send.at[k], c_recv.at[k], sibling)
        yield
        copy.wait_recv()
        so[k] = (outs[k, C].astype(F32) + core[k].astype(F32)).astype(BF16)
        copies = []
        for j in (2, 1, 3):
            copies.append(send(
                so.at[k, share(X + j)], xr.at[k, j - 1], xr_send.at[k, j - 1], xr_recv.at[k, j - 1], at(X + j, Y)
            ))
        yield
        for copy in copies:
            copy.wait_recv()
        total = so[k, share(X)].astype(F32)
        for j in range(NX - 1):
            total += xr[k, j].astype(F32)
        if k == 0:
            got[0] = total.astype(BF16)
            return
        zs[k] = total.astype(BF16)
        o_copies[BACK[k]] = send(
            zs.at[k], got.at[BACK[k]], o_send.at[k], o_recv.at[BACK[k]], (dp, lax.rem(e + 2 * off, N_EXPERT))
        )

    chunks = [chunk(k) for k in range(NZ)]
    for k in plan():
        next(chunks[k], None)

    for key in sorted(o_copies):
        o_copies[key].wait_recv()
    total = jnp.zeros((SHARE, SPAN), F32)
    for k in range(NZ):
        total += got[k].astype(F32)
    total = total.astype(BF16)
    stacked = jnp.concatenate([total[:, g * 128:(g + 1) * 128] for g in range(GROUPS)], axis=0)
    m = lax.broadcasted_iota(jnp.int32, (NY * 16, GROUPS * 16), 0)
    n = lax.broadcasted_iota(jnp.int32, (NY * 16, GROUPS * 16), 1)
    place = (((m >> 1) & 7) * 16 + (m >> 4) * 2 + (m & 1) == n).astype(BF16)
    moved = jnp.dot(place, stacked, preferred_element_type=F32).astype(BF16)
    fin_src[...] = moved.reshape(NY, 16, 128)
    copies = []
    for j in FAR_FIRST:
        y = lax.rem(Y + j, NY)
        copies.append(send(fin_src.at[y], fin.at[Y], f_send.at[j - 1], f_recv.at[j - 1], at(X, y)))
    fin[Y] = fin_src[Y]
    for copy in copies:
        copy.wait_recv()
    pieces = []
    for y in range(NY):
        tile = fin[y].astype(F32)
        pieces += [tile[2 * g:2 * g + 2] for g in range(GROUPS)]
    out_ref[...] = jnp.concatenate(pieces, axis=1).astype(BF16)
    for copy in sends:
        copy.wait_send()


def shards(tokens, w_gate, w_up, w_down, routes, scores):
    dma = pltpu.SemaphoreType.DMA
    vmem = pltpu.VMEM
    return pl.pallas_call(
        kernel,
        out_shape=jax.ShapeDtypeStruct(tokens.shape, BF16),
        in_specs=[pl.BlockSpec(memory_space=pl.ANY)] * 6,
        out_specs=pl.BlockSpec(memory_space=vmem),
        scratch_shapes=[
            vmem(tokens.shape, tokens.dtype),
            vmem(routes.shape, routes.dtype),
            vmem(scores.shape, scores.dtype),
            vmem((SPAN, 2 * UNITS), BF16),
            vmem((SPAN, UNITS), BF16),
            vmem((NY, 16, 128), BF16),
            vmem((NY, 16, 128), BF16),
            vmem((N_EXPERT, ROWS, PAD), BF16),
            vmem((NZ, CHUNK, 2 * UNITS), BF16),
            vmem((NZ, NY - 1, STRIP, 2 * UNITS), BF16),
            vmem((NZ, CHUNK, UNITS), BF16),
            vmem((NZ, 2, ROWS, SPAN), BF16),
            vmem((NZ, ROWS, SPAN), BF16),
            vmem((NZ, ROWS, SPAN), BF16),
            vmem((NZ, NX - 1, SHARE, SPAN), BF16),
            vmem((NZ, SHARE, SPAN), BF16),
            vmem((NZ, SHARE, SPAN), BF16),
            vmem((NY, 16, 128), BF16),
            vmem((NY, 16, 128), BF16),
            dma((3,)),
            dma((NY - 1,)),
            dma((NY - 1,)),
            dma((3, NX)),
            dma((3, NX)),
            dma((NZ,)),
            dma((NZ,)),
            dma((NZ, NX - 1)),
            dma((NZ, NX - 1)),
            dma((NZ,)),
            dma((NZ,)),
            dma((NZ, NY - 1)),
            dma((NZ, NY - 1)),
            dma((NZ, NY - 1)),
            dma((NZ, NY - 1)),
            dma((NZ,)),
            dma((NZ,)),
            dma((NZ, NX - 1)),
            dma((NZ, NX - 1)),
            dma((NZ,)),
            dma((NZ,)),
            dma((NY - 1,)),
            dma((NY - 1,)),
        ],
        compiler_params=pltpu.CompilerParams(
            collective_id=0, has_side_effects=True, vmem_limit_bytes=56 * 1024 * 1024
        ),
        name="expert_block",
    )(tokens, routes, scores, w_gate, w_up, w_down.swapaxes(1, 2))


def solution(mesh):
    placed = (
        P(("dp", "expert"), None),
        P("expert", "dp", None),
        P("expert", "dp", None),
        P("expert", None, "dp"),
        P(("dp", "expert"), None),
        P(("dp", "expert"), None),
    )
    return jax.shard_map(
        shards, mesh=mesh, in_specs=placed, out_specs=P(("dp", "expert"), None), check_vma=False
    )
```

```python
import jax
import jax.numpy as jnp
from jax import lax
from jax.experimental import pallas as pl
from jax.experimental.pallas import tpu as pltpu
from jax.sharding import PartitionSpec as P

MESH = pl.DeviceIdType.MESH
F32 = jnp.float32
BF16 = jnp.bfloat16

ROUTE_SCALE = 2.5
NX, NY, NZ = 4, 8, 8
N_DP = NX * NY
N_EXPERT = 2 * NZ
D = 7168
WIDTH = D // N_DP
FFW = 1024
SPAN = NX * WIDTH
GROUPS = SPAN // 128
PAD = SPAN + 128
ROWS = 64
CHUNK = 2 * ROWS
UNITS = FFW // NX
STRIP = CHUNK // NY
SHARE = ROWS // NX
OFFSETS = (0, 1, 4, 3, 5, 2, 6, 7)
BACK = tuple(OFFSETS.index((NZ - o) % NZ) for o in OFFSETS)
STRAIGHT = ()
FAR_FIRST = (4, 3, 5, 2, 6, 1, 7)
LATEST = 16
FROM_Z = (9.3, 13.3, 15.8, 16.6, 16.9, 17.4, 17.7, 18.0)
FROM_X = (15, 17.5, 20, 21, 21.8, 22.8, 23.8, 24.8)
START = (16.6, 18.9, 21.4, 22.4, 23.2, 24.2, 25.6, 27.1)
HOP = 3.8


def plan():
    events = []
    for k in range(NZ):
        times = [FROM_Z[k], FROM_X[k], START[k]]
        waits = (1.5 * HOP, 1.3 * HOP) if k in STRAIGHT else (HOP,) * 4
        for wait in waits + (1.6, HOP):
            times.append(times[-1] + wait)
        events += [(when, k) for when in times]
    return [k for _, k in sorted(events)]


def kernel(
    tok_hbm, routes_hbm, scores_hbm, wg_hbm, wu_hbm, wd_hbm, out_ref,
    tok_ref, routes_ref, scores_ref, w_in, w_out, tok_src, mail, xall, part, rs, hid, outs, core, so, xr, zs, got, fin_src, fin,
    in_sem, m_send, m_recv, w_send, w_recv, z_send, z_recv, x_send, x_recv, s_send, s_recv, rs_send, rs_recv, ag_send, ag_recv,
    c_send, c_recv, xr_send, xr_recv, o_send, o_recv, f_send, f_recv,
):
    dp = lax.axis_index("dp")
    e = lax.axis_index("expert")
    X, Y = dp % NX, dp // NX
    Z, C = e // 2, e % 2
    sibling = (dp, Z * 2 + (C + 1) % 2)

    def at(x, y):
        return (lax.rem(y, NY) * NX + lax.rem(x, NX), e)

    loads = [
        pltpu.make_async_copy(src, dst, in_sem.at[n])
        for n, (src, dst) in enumerate(((tok_hbm, tok_ref), (routes_hbm, routes_ref), (scores_hbm, scores_ref)))
    ]
    for load in loads:
        load.start()

    barrier = pltpu.get_barrier_semaphore()

    peers = [at(X, Y + j) for j in range(1, NY)] + [sibling]
    peers += [at(X + j, Y) for j in range(1, NX)] + [(dp, lax.rem(e + 2 * j, N_EXPERT)) for j in range(1, NZ)]
    for peer in peers:
        pl.semaphore_signal(barrier, inc=1, device_id=peer, device_id_type=MESH)

    pl.semaphore_wait(barrier, len(peers))

    sends = []

    def send(src, dst, send_sem, recv_sem, device):
        copy = pltpu.make_async_remote_copy(src, dst, send_sem, recv_sem, device_id=device, device_id_type=MESH)
        copy.start()
        sends.append(copy)
        return copy

    w_copies = []
    block = pl.ds(pl.multiple_of(X * WIDTH, 16), WIDTH)
    homes = (w_in.at[block, pl.ds(0, UNITS)], w_in.at[block, pl.ds(UNITS, UNITS)], w_out.at[block])

    def give(n, src, b):
        for j in (2, 1, 3, 0):
            x = lax.rem(X + j, NX)
            a = src.at[0, :, pl.ds(pl.multiple_of(x * UNITS, UNITS), UNITS)]
            if j == 0:
                copy = pltpu.make_async_copy(a, b, w_recv.at[n, 0])
                copy.start()
                w_copies.append((n, copy.wait))
            else:
                copy = send(a, b, w_send.at[n, j], w_recv.at[n, j], at(x, Y))
                w_copies.append((n, copy.wait_recv))

    give(0, wg_hbm, homes[0])
    give(1, wu_hbm, homes[1])

    for load in loads:
        load.wait()
    scores = scores_ref[...]
    weights = ROUTE_SCALE * scores / jnp.sum(scores, axis=1, keepdims=True)
    routes = routes_ref[...]
    lanes = lax.broadcasted_iota(jnp.int32, (2, 128), 1)
    table = jnp.zeros((2, 128), F32)
    for k in range(routes.shape[1]):
        table += jnp.where(routes[:, k:k + 1] == (lanes & (N_EXPERT - 1)), weights[:, k:k + 1], 0.0)
    high = table.astype(BF16).astype(F32)
    extra = jnp.where(lanes < N_EXPERT, high, jnp.where(lanes < 2 * N_EXPERT, table - high, 0.0))
    tokens = tok_ref[...].astype(F32)
    for y in range(NY):
        pieces = [tokens[:, y * SPAN + g * 128:y * SPAN + (g + 1) * 128] for g in range(GROUPS)]
        tok_src[y] = jnp.concatenate(pieces + [extra], axis=0).astype(BF16)

    mail_copies = []
    for j in FAR_FIRST:
        y = lax.rem(Y + j, NY)
        mail_copies.append(send(tok_src.at[y], mail.at[Y], m_send.at[j - 1], m_recv.at[j - 1], at(X, y)))
    mail[Y] = tok_src[Y]

    size = NY * 16
    m = lax.broadcasted_iota(jnp.int32, (size, size), 0)
    n = lax.broadcasted_iota(jnp.int32, (size, size), 1)
    pick = (((m >> 1) & 7) * 16 + (m >> 4) * 2 + (m & 1) == n).astype(BF16)
    for copy in mail_copies:
        copy.wait_recv()
    rows = jnp.dot(pick, mail[...].reshape(size, 128), preferred_element_type=F32).astype(BF16)

    def share(x):
        return pl.ds(pl.multiple_of(lax.rem(x, NX) * SHARE, SHARE), SHARE)

    for g in range(GROUPS + 1):
        xall[e, share(X), pl.ds(g * 128, 128)] = rows[g * SHARE:(g + 1) * SHARE]

    own = xall.at[e, share(X)]
    z_copies = {}
    for k in range(1, NZ):
        there = (dp, lax.rem(e + 2 * OFFSETS[k], N_EXPERT))
        z_copies[BACK[k]] = send(own, own, z_send.at[k], z_recv.at[BACK[k]], there)

    lane = lax.broadcasted_iota(jnp.int32, (CHUNK, 128), 1)
    mine = (lane == e) | (lane == N_EXPERT + e)
    o_copies = {}

    def ready(n):
        for kind, wait in w_copies:
            if kind == n:
                wait()

    def strip(y):
        return pl.ds(pl.multiple_of(lax.rem(y, NY) * STRIP, STRIP), STRIP)

    def sum_send(k, n, src, j):
        return send(src, rs.at[k, n], rs_send.at[k, n], rs_recv.at[k, n], at(X, Y + j + NY))

    def sum_straight(k):
        copies = [sum_send(k, j - 1, part.at[k, strip(Y + j)], j) for j in FAR_FIRST]
        yield
        for copy in copies:
            copy.wait_recv()

    def sum_tree(k, t):
        def piece(j):
            return part.at[k, strip(Y + j + NY)]

        a = sum_send(k, 0, piece(4), 2 * t)
        b = sum_send(k, 1, piece(3 * t), t)
        c = sum_send(k, 2, piece(-3 * t), -t)
        last = [sum_send(k, 3, piece(t), t), sum_send(k, 4, piece(-t), -t)]
        yield
        c.wait_recv()
        rs[k, 2] = (rs[k, 2].astype(F32) + piece(-2 * t)[...].astype(F32)).astype(BF16)
        last.append(sum_send(k, 5, rs.at[k, 2], -2 * t))
        a.wait_recv()
        b.wait_recv()
        total = rs[k, 0].astype(F32) + rs[k, 1].astype(F32) + piece(2 * t)[...].astype(F32)
        rs[k, 0] = total.astype(BF16)
        last.append(sum_send(k, 6, rs.at[k, 0], 2 * t))
        yield
        for copy in last:
            copy.wait_recv()

    def gather_send(k, n, source, j):
        ref = hid.at[k, strip(Y + source + NY)]
        return send(ref, ref, ag_send.at[k, n], ag_recv.at[k, n], at(X, Y + j + NY))

    def gather_straight(k):
        copies = [gather_send(k, j - 1, 0, j) for j in FAR_FIRST]
        yield
        for copy in copies:
            copy.wait_recv()

    def gather_tree(k, t):
        a = gather_send(k, 0, 0, 2 * t)
        b = gather_send(k, 1, 0, -2 * t)
        last = [gather_send(k, 2, 0, t), gather_send(k, 3, 0, -t)]
        yield
        a.wait_recv()
        last.append(gather_send(k, 4, -2 * t, 2 * t))
        last.append(gather_send(k, 5, -2 * t, t))
        b.wait_recv()
        last.append(gather_send(k, 6, 2 * t, -t))
        yield
        for copy in last:
            copy.wait_recv()

    def chunk(k):
        off = OFFSETS[k]
        zc = (Z + off) % NZ
        block = zc * 2 + C
        if k > 0:
            z_copies[k].wait_recv()
        rows = xall.at[block, share(X)]
        copies = []
        for j in (2, 1, 3):
            copies.append(send(rows, rows, x_send.at[k, j - 1], x_recv.at[k, j - 1], at(X + j, Y)))
        if k == NZ - 1:
            give(2, wd_hbm, homes[2])
        yield
        for copy in copies:
            copy.wait_recv()
        copy = send(xall.at[block], xall.at[block], s_send.at[k], s_recv.at[k], sibling)
        yield
        copy.wait_recv()
        if k == 0:
            ready(0)
            ready(1)
        x = xall[pl.ds(2 * zc, 2), :, 0:SPAN].reshape(CHUNK, SPAN)
        part[k] = jnp.dot(x, w_in[...], preferred_element_type=F32).astype(BF16)
        turn = 1 if k % 2 == 0 else -1
        if k in STRAIGHT:
            yield from sum_straight(k)
            parts = [rs[k, j] for j in range(NY - 1)]
        else:
            yield from sum_tree(k, turn)
            parts = [rs[k, j] for j in (3, 4, 5, 6)]
        total = part[k, strip(Y)].astype(F32)
        for value in parts:
            total += value.astype(F32)
        gate, up_ = total[:, :UNITS], total[:, UNITS:]
        hid[k, strip(Y)] = (gate / (1.0 + jnp.exp(-gate)) * up_).astype(BF16)
        if k in STRAIGHT:
            yield from gather_straight(k)
        else:
            yield from gather_tree(k, turn)
        if k == 0:
            ready(2)
        extra = xall[pl.ds(2 * zc, 2), :, SPAN:].reshape(CHUNK, 128).astype(F32)
        weight = jnp.sum(jnp.where(mine, extra, 0.0), axis=1, keepdims=True)
        o = lax.dot_general(hid[k], w_out[...], (((1,), (1,)), ((), ())), preferred_element_type=F32)
        outs[k] = (o * weight).astype(BF16).reshape(2, ROWS, SPAN)
        copy = send(outs.at[k, lax.rem(C + 1, 2)], core.at[k], c_send.at[k], c_recv.at[k], sibling)
        yield
        copy.wait_recv()
        so[k] = (outs[k, C].astype(F32) + core[k].astype(F32)).astype(BF16)
        copies = []
        for j in (2, 1, 3):
            copies.append(send(
                so.at[k, share(X + j)], xr.at[k, j - 1], xr_send.at[k, j - 1], xr_recv.at[k, j - 1], at(X + j, Y)
            ))
        yield
        for copy in copies:
            copy.wait_recv()
        total = so[k, share(X)].astype(F32)
        for j in range(NX - 1):
            total += xr[k, j].astype(F32)
        if k == 0:
            got[0] = total.astype(BF16)
            return
        zs[k] = total.astype(BF16)
        o_copies[BACK[k]] = send(
            zs.at[k], got.at[BACK[k]], o_send.at[k], o_recv.at[BACK[k]], (dp, lax.rem(e + 2 * off, N_EXPERT))
        )

    chunks = [chunk(k) for k in range(NZ)]
    for k in plan():
        next(chunks[k], None)

    m = lax.broadcasted_iota(jnp.int32, (NY * 16, GROUPS * 16), 0)
    n = lax.broadcasted_iota(jnp.int32, (NY * 16, GROUPS * 16), 1)
    place = (((m >> 1) & 7) * 16 + (m >> 4) * 2 + (m & 1) == n).astype(BF16)
    settled = len(sends) - LATEST
    for copy in sends[:settled]:
        copy.wait_send()
    for key in sorted(o_copies):
        o_copies[key].wait_recv()
    total = jnp.zeros((SHARE, SPAN), F32)
    for k in range(NZ):
        total += got[k].astype(F32)
    total = total.astype(BF16)
    stacked = jnp.concatenate([total[:, g * 128:(g + 1) * 128] for g in range(GROUPS)], axis=0)
    moved = jnp.dot(place, stacked, preferred_element_type=F32).astype(BF16)
    fin_src[...] = moved.reshape(NY, 16, 128)
    copies = []
    for j in FAR_FIRST:
        y = lax.rem(Y + j, NY)
        copies.append(send(fin_src.at[y], fin.at[Y], f_send.at[j - 1], f_recv.at[j - 1], at(X, y)))
    fin[Y] = fin_src[Y]
    for copy in sends[settled:-len(copies)]:
        copy.wait_send()
    for copy in copies:
        copy.wait_recv()
    pieces = []
    for y in range(NY):
        tile = fin[y].astype(F32)
        pieces += [tile[2 * g:2 * g + 2] for g in range(GROUPS)]
    out_ref[...] = jnp.concatenate(pieces, axis=1).astype(BF16)
    for copy in copies:
        copy.wait_send()


def shards(tokens, w_gate, w_up, w_down, routes, scores):
    dma = pltpu.SemaphoreType.DMA
    vmem = pltpu.VMEM
    return pl.pallas_call(
        kernel,
        out_shape=jax.ShapeDtypeStruct(tokens.shape, BF16),
        in_specs=[pl.BlockSpec(memory_space=pl.ANY)] * 6,
        out_specs=pl.BlockSpec(memory_space=vmem),
        scratch_shapes=[
            vmem(tokens.shape, tokens.dtype),
            vmem(routes.shape, routes.dtype),
            vmem(scores.shape, scores.dtype),
            vmem((SPAN, 2 * UNITS), BF16),
            vmem((SPAN, UNITS), BF16),
            vmem((NY, 16, 128), BF16),
            vmem((NY, 16, 128), BF16),
            vmem((N_EXPERT, ROWS, PAD), BF16),
            vmem((NZ, CHUNK, 2 * UNITS), BF16),
            vmem((NZ, NY - 1, STRIP, 2 * UNITS), BF16),
            vmem((NZ, CHUNK, UNITS), BF16),
            vmem((NZ, 2, ROWS, SPAN), BF16),
            vmem((NZ, ROWS, SPAN), BF16),
            vmem((NZ, ROWS, SPAN), BF16),
            vmem((NZ, NX - 1, SHARE, SPAN), BF16),
            vmem((NZ, SHARE, SPAN), BF16),
            vmem((NZ, SHARE, SPAN), BF16),
            vmem((NY, 16, 128), BF16),
            vmem((NY, 16, 128), BF16),
            dma((3,)),
            dma((NY - 1,)),
            dma((NY - 1,)),
            dma((3, NX)),
            dma((3, NX)),
            dma((NZ,)),
            dma((NZ,)),
            dma((NZ, NX - 1)),
            dma((NZ, NX - 1)),
            dma((NZ,)),
            dma((NZ,)),
            dma((NZ, NY - 1)),
            dma((NZ, NY - 1)),
            dma((NZ, NY - 1)),
            dma((NZ, NY - 1)),
            dma((NZ,)),
            dma((NZ,)),
            dma((NZ, NX - 1)),
            dma((NZ, NX - 1)),
            dma((NZ,)),
            dma((NZ,)),
            dma((NY - 1,)),
            dma((NY - 1,)),
        ],
        compiler_params=pltpu.CompilerParams(
            collective_id=0, has_side_effects=True, vmem_limit_bytes=56 * 1024 * 1024
        ),
        name="expert_block",
    )(tokens, routes, scores, w_gate, w_up, w_down.swapaxes(1, 2))


def solution(mesh):
    placed = (
        P(("dp", "expert"), None),
        P("expert", "dp", None),
        P("expert", "dp", None),
        P("expert", None, "dp"),
        P(("dp", "expert"), None),
        P(("dp", "expert"), None),
    )
    return jax.shard_map(
        shards, mesh=mesh, in_specs=placed, out_specs=P(("dp", "expert"), None), check_vma=False
    )
```

```python
import jax
import jax.numpy as jnp
from jax import lax
from jax.experimental import pallas as pl
from jax.experimental.pallas import tpu as pltpu
from jax.sharding import PartitionSpec as P

MESH = pl.DeviceIdType.MESH
F32 = jnp.float32
BF16 = jnp.bfloat16

ROUTE_SCALE = 2.5
NX, NY, NZ = 4, 8, 8
N_DP = NX * NY
N_EXPERT = 2 * NZ
D = 7168
WIDTH = D // N_DP
FFW = 1024
SPAN = NX * WIDTH
GROUPS = SPAN // 128
PAD = SPAN + 128
ROWS = 64
CHUNK = 2 * ROWS
UNITS = FFW // NX
STRIP = CHUNK // NY
SHARE = ROWS // NX
OFFSETS = (0, 1, 4, 3, 5, 2, 6, 7)
BACK = tuple(OFFSETS.index((NZ - o) % NZ) for o in OFFSETS)
STRAIGHT = ()
FAR_FIRST = (4, 3, 5, 2, 6, 1, 7)
LATEST = 16
FROM_Z = (9.3, 13.3, 15.8, 16.6, 16.9, 17.4, 17.7, 18.0)
FROM_X = (15, 17.5, 20, 21, 21.8, 22.8, 23.8, 24.8)
START = (16.6, 18.9, 21.4, 22.4, 23.2, 24.2, 25.6, 27.1)
HOP = 3.8


def plan():
    events = []
    for k in range(NZ):
        times = [FROM_Z[k], FROM_X[k], START[k]]
        waits = (1.5 * HOP, 1.3 * HOP) if k in STRAIGHT else (HOP,) * 4
        for wait in waits + (1.6, HOP):
            times.append(times[-1] + wait)
        events += [(when, k) for when in times]
    return [k for _, k in sorted(events)]


def kernel(
    tok_hbm, routes_hbm, scores_hbm, wg_hbm, wu_hbm, wd_hbm, out_ref,
    tok_ref, routes_ref, scores_ref, w_in, w_out, tok_src, mail, xall, part, rs, hid, outs, core, so, xr, zs, got, fin_src, fin,
    in_sem, m_send, m_recv, w_send, w_recv, z_send, z_recv, x_send, x_recv, s_send, s_recv, rs_send, rs_recv, ag_send, ag_recv,
    c_send, c_recv, xr_send, xr_recv, o_send, o_recv, f_send, f_recv,
):
    dp = lax.axis_index("dp")
    e = lax.axis_index("expert")
    X, Y = dp % NX, dp // NX
    Z, C = e // 2, e % 2
    sibling = (dp, Z * 2 + (C + 1) % 2)

    def at(x, y):
        return (lax.rem(y, NY) * NX + lax.rem(x, NX), e)

    loads = [
        pltpu.make_async_copy(src, dst, in_sem.at[n])
        for n, (src, dst) in enumerate(((tok_hbm, tok_ref), (routes_hbm, routes_ref), (scores_hbm, scores_ref)))
    ]
    for load in loads:
        load.start()

    barrier = pltpu.get_barrier_semaphore()

    peers = []
    for j in (4, 3, 5, 2, 6, 1, 7):
        peers += [at(X, Y + j), (dp, lax.rem(e + 2 * j, N_EXPERT))]
    peers += [at(X + j, Y) for j in (2, 1, 3)] + [sibling]
    for peer in peers:
        pl.semaphore_signal(barrier, inc=1, device_id=peer, device_id_type=MESH)

    pl.semaphore_wait(barrier, len(peers))

    sends = []

    def send(src, dst, send_sem, recv_sem, device):
        copy = pltpu.make_async_remote_copy(src, dst, send_sem, recv_sem, device_id=device, device_id_type=MESH)
        copy.start()
        sends.append(copy)
        return copy

    w_copies = []
    block = pl.ds(pl.multiple_of(X * WIDTH, 16), WIDTH)
    homes = (w_in.at[block, pl.ds(0, UNITS)], w_in.at[block, pl.ds(UNITS, UNITS)], w_out.at[block])

    def give(n, src, b):
        for j in (2, 1, 3, 0):
            x = lax.rem(X + j, NX)
            a = src.at[0, :, pl.ds(pl.multiple_of(x * UNITS, UNITS), UNITS)]
            if j == 0:
                copy = pltpu.make_async_copy(a, b, w_recv.at[n, 0])
                copy.start()
                w_copies.append((n, copy.wait))
            else:
                copy = send(a, b, w_send.at[n, j], w_recv.at[n, j], at(x, Y))
                w_copies.append((n, copy.wait_recv))

    give(0, wg_hbm, homes[0])
    give(1, wu_hbm, homes[1])

    for load in loads:
        load.wait()
    scores = scores_ref[...]
    weights = ROUTE_SCALE * scores / jnp.sum(scores, axis=1, keepdims=True)
    routes = routes_ref[...]
    lanes = lax.broadcasted_iota(jnp.int32, (2, 128), 1)
    table = jnp.zeros((2, 128), F32)
    for k in range(routes.shape[1]):
        table += jnp.where(routes[:, k:k + 1] == (lanes & (N_EXPERT - 1)), weights[:, k:k + 1], 0.0)
    high = table.astype(BF16).astype(F32)
    extra = jnp.where(lanes < N_EXPERT, high, jnp.where(lanes < 2 * N_EXPERT, table - high, 0.0))
    tokens = tok_ref[...].astype(F32)
    for y in range(NY):
        pieces = [tokens[:, y * SPAN + g * 128:y * SPAN + (g + 1) * 128] for g in range(GROUPS)]
        tok_src[y] = jnp.concatenate(pieces + [extra], axis=0).astype(BF16)

    mail_copies = []
    for j in FAR_FIRST:
        y = lax.rem(Y + j, NY)
        mail_copies.append(send(tok_src.at[y], mail.at[Y], m_send.at[j - 1], m_recv.at[j - 1], at(X, y)))
    mail[Y] = tok_src[Y]

    size = NY * 16
    m = lax.broadcasted_iota(jnp.int32, (size, size), 0)
    n = lax.broadcasted_iota(jnp.int32, (size, size), 1)
    pick = (((m >> 1) & 7) * 16 + (m >> 4) * 2 + (m & 1) == n).astype(BF16)
    for copy in mail_copies:
        copy.wait_recv()
    rows = jnp.dot(pick, mail[...].reshape(size, 128), preferred_element_type=F32).astype(BF16)

    def share(x):
        return pl.ds(pl.multiple_of(lax.rem(x, NX) * SHARE, SHARE), SHARE)

    for g in range(GROUPS + 1):
        xall[e, share(X), pl.ds(g * 128, 128)] = rows[g * SHARE:(g + 1) * SHARE]

    own = xall.at[e, share(X)]
    z_copies = {}
    for k in range(1, NZ):
        there = (dp, lax.rem(e + 2 * OFFSETS[k], N_EXPERT))
        z_copies[BACK[k]] = send(own, own, z_send.at[k], z_recv.at[BACK[k]], there)

    lane = lax.broadcasted_iota(jnp.int32, (CHUNK, 128), 1)
    mine = (lane == e) | (lane == N_EXPERT + e)
    o_copies = {}

    def ready(n):
        for kind, wait in w_copies:
            if kind == n:
                wait()

    def strip(y):
        return pl.ds(pl.multiple_of(lax.rem(y, NY) * STRIP, STRIP), STRIP)

    def sum_send(k, n, src, j):
        return send(src, rs.at[k, n], rs_send.at[k, n], rs_recv.at[k, n], at(X, Y + j + NY))

    def sum_straight(k):
        copies = [sum_send(k, j - 1, part.at[k, strip(Y + j)], j) for j in FAR_FIRST]
        yield
        for copy in copies:
            copy.wait_recv()

    def sum_tree(k, t):
        def piece(j):
            return part.at[k, strip(Y + j + NY)]

        a = sum_send(k, 0, piece(4), 2 * t)
        b = sum_send(k, 1, piece(3 * t), t)
        c = sum_send(k, 2, piece(-3 * t), -t)
        last = [sum_send(k, 3, piece(t), t), sum_send(k, 4, piece(-t), -t)]
        yield
        c.wait_recv()
        rs[k, 2] = (rs[k, 2].astype(F32) + piece(-2 * t)[...].astype(F32)).astype(BF16)
        last.append(sum_send(k, 5, rs.at[k, 2], -2 * t))
        a.wait_recv()
        b.wait_recv()
        total = rs[k, 0].astype(F32) + rs[k, 1].astype(F32) + piece(2 * t)[...].astype(F32)
        rs[k, 0] = total.astype(BF16)
        last.append(sum_send(k, 6, rs.at[k, 0], 2 * t))
        yield
        for copy in last:
            copy.wait_recv()

    def gather_send(k, n, source, j):
        ref = hid.at[k, strip(Y + source + NY)]
        return send(ref, ref, ag_send.at[k, n], ag_recv.at[k, n], at(X, Y + j + NY))

    def gather_straight(k):
        copies = [gather_send(k, j - 1, 0, j) for j in FAR_FIRST]
        yield
        for copy in copies:
            copy.wait_recv()

    def gather_tree(k, t):
        a = gather_send(k, 0, 0, 2 * t)
        b = gather_send(k, 1, 0, -2 * t)
        last = [gather_send(k, 2, 0, t), gather_send(k, 3, 0, -t)]
        yield
        a.wait_recv()
        last.append(gather_send(k, 4, -2 * t, 2 * t))
        last.append(gather_send(k, 5, -2 * t, t))
        b.wait_recv()
        last.append(gather_send(k, 6, 2 * t, -t))
        yield
        for copy in last:
            copy.wait_recv()

    def chunk(k):
        off = OFFSETS[k]
        zc = (Z + off) % NZ
        block = zc * 2 + C
        if k > 0:
            z_copies[k].wait_recv()
        rows = xall.at[block, share(X)]
        copies = []
        for j in (2, 1, 3):
            copies.append(send(rows, rows, x_send.at[k, j - 1], x_recv.at[k, j - 1], at(X + j, Y)))
        if k == NZ - 1:
            give(2, wd_hbm, homes[2])
        yield
        for copy in copies:
            copy.wait_recv()
        copy = send(xall.at[block], xall.at[block], s_send.at[k], s_recv.at[k], sibling)
        yield
        copy.wait_recv()
        if k == 0:
            ready(0)
            ready(1)
        x = xall[pl.ds(2 * zc, 2), :, 0:SPAN].reshape(CHUNK, SPAN)
        part[k] = jnp.dot(x, w_in[...], preferred_element_type=F32).astype(BF16)
        turn = 1 if k % 2 == 0 else -1
        if k in STRAIGHT:
            yield from sum_straight(k)
            parts = [rs[k, j] for j in range(NY - 1)]
        else:
            yield from sum_tree(k, turn)
            parts = [rs[k, j] for j in (3, 4, 5, 6)]
        total = part[k, strip(Y)].astype(F32)
        for value in parts:
            total += value.astype(F32)
        gate, up_ = total[:, :UNITS], total[:, UNITS:]
        hid[k, strip(Y)] = (gate / (1.0 + jnp.exp(-gate)) * up_).astype(BF16)
        if k in STRAIGHT:
            yield from gather_straight(k)
        else:
            yield from gather_tree(k, turn)
        if k == 0:
            ready(2)
        extra = xall[pl.ds(2 * zc, 2), :, SPAN:].reshape(CHUNK, 128).astype(F32)
        weight = jnp.sum(jnp.where(mine, extra, 0.0), axis=1, keepdims=True)
        o = lax.dot_general(hid[k], w_out[...], (((1,), (1,)), ((), ())), preferred_element_type=F32)
        outs[k] = (o * weight).astype(BF16).reshape(2, ROWS, SPAN)
        copy = send(outs.at[k, lax.rem(C + 1, 2)], core.at[k], c_send.at[k], c_recv.at[k], sibling)
        yield
        copy.wait_recv()
        so[k] = (outs[k, C].astype(F32) + core[k].astype(F32)).astype(BF16)
        copies = []
        for j in (2, 1, 3):
            copies.append(send(
                so.at[k, share(X + j)], xr.at[k, j - 1], xr_send.at[k, j - 1], xr_recv.at[k, j - 1], at(X + j, Y)
            ))
        yield
        for copy in copies:
            copy.wait_recv()
        total = so[k, share(X)].astype(F32)
        for j in range(NX - 1):
            total += xr[k, j].astype(F32)
        if k == 0:
            got[0] = total.astype(BF16)
            return
        zs[k] = total.astype(BF16)
        o_copies[BACK[k]] = send(
            zs.at[k], got.at[BACK[k]], o_send.at[k], o_recv.at[BACK[k]], (dp, lax.rem(e + 2 * off, N_EXPERT))
        )

    chunks = [chunk(k) for k in range(NZ)]
    for k in plan():
        next(chunks[k], None)

    m = lax.broadcasted_iota(jnp.int32, (NY * 16, GROUPS * 16), 0)
    n = lax.broadcasted_iota(jnp.int32, (NY * 16, GROUPS * 16), 1)
    place = (((m >> 1) & 7) * 16 + (m >> 4) * 2 + (m & 1) == n).astype(BF16)
    settled = len(sends) - LATEST
    for copy in sends[:settled]:
        copy.wait_send()
    for key in sorted(o_copies):
        o_copies[key].wait_recv()
    total = jnp.zeros((SHARE, SPAN), F32)
    for k in range(NZ):
        total += got[k].astype(F32)
    total = total.astype(BF16)
    stacked = jnp.concatenate([total[:, g * 128:(g + 1) * 128] for g in range(GROUPS)], axis=0)
    moved = jnp.dot(place, stacked, preferred_element_type=F32).astype(BF16)
    fin_src[...] = moved.reshape(NY, 16, 128)
    copies = []
    for j in FAR_FIRST:
        y = lax.rem(Y + j, NY)
        copies.append(send(fin_src.at[y], fin.at[Y], f_send.at[j - 1], f_recv.at[j - 1], at(X, y)))
    fin[Y] = fin_src[Y]
    for copy in sends[settled:-len(copies)]:
        copy.wait_send()
    for copy in copies:
        copy.wait_recv()
    pieces = []
    for y in range(NY):
        tile = fin[y].astype(F32)
        pieces += [tile[2 * g:2 * g + 2] for g in range(GROUPS)]
    out_ref[...] = jnp.concatenate(pieces, axis=1).astype(BF16)
    for copy in copies:
        copy.wait_send()


def shards(tokens, w_gate, w_up, w_down, routes, scores):
    dma = pltpu.SemaphoreType.DMA
    vmem = pltpu.VMEM
    return pl.pallas_call(
        kernel,
        out_shape=jax.ShapeDtypeStruct(tokens.shape, BF16),
        in_specs=[pl.BlockSpec(memory_space=pl.ANY)] * 6,
        out_specs=pl.BlockSpec(memory_space=vmem),
        scratch_shapes=[
            vmem(tokens.shape, tokens.dtype),
            vmem(routes.shape, routes.dtype),
            vmem(scores.shape, scores.dtype),
            vmem((SPAN, 2 * UNITS), BF16),
            vmem((SPAN, UNITS), BF16),
            vmem((NY, 16, 128), BF16),
            vmem((NY, 16, 128), BF16),
            vmem((N_EXPERT, ROWS, PAD), BF16),
            vmem((NZ, CHUNK, 2 * UNITS), BF16),
            vmem((NZ, NY - 1, STRIP, 2 * UNITS), BF16),
            vmem((NZ, CHUNK, UNITS), BF16),
            vmem((NZ, 2, ROWS, SPAN), BF16),
            vmem((NZ, ROWS, SPAN), BF16),
            vmem((NZ, ROWS, SPAN), BF16),
            vmem((NZ, NX - 1, SHARE, SPAN), BF16),
            vmem((NZ, SHARE, SPAN), BF16),
            vmem((NZ, SHARE, SPAN), BF16),
            vmem((NY, 16, 128), BF16),
            vmem((NY, 16, 128), BF16),
            dma((3,)),
            dma((NY - 1,)),
            dma((NY - 1,)),
            dma((3, NX)),
            dma((3, NX)),
            dma((NZ,)),
            dma((NZ,)),
            dma((NZ, NX - 1)),
            dma((NZ, NX - 1)),
            dma((NZ,)),
            dma((NZ,)),
            dma((NZ, NY - 1)),
            dma((NZ, NY - 1)),
            dma((NZ, NY - 1)),
            dma((NZ, NY - 1)),
            dma((NZ,)),
            dma((NZ,)),
            dma((NZ, NX - 1)),
            dma((NZ, NX - 1)),
            dma((NZ,)),
            dma((NZ,)),
            dma((NY - 1,)),
            dma((NY - 1,)),
        ],
        compiler_params=pltpu.CompilerParams(
            collective_id=0, has_side_effects=True, vmem_limit_bytes=56 * 1024 * 1024
        ),
        name="expert_block",
    )(tokens, routes, scores, w_gate, w_up, w_down.swapaxes(1, 2))


def solution(mesh):
    placed = (
        P(("dp", "expert"), None),
        P("expert", "dp", None),
        P("expert", "dp", None),
        P("expert", None, "dp"),
        P(("dp", "expert"), None),
        P(("dp", "expert"), None),
    )
    return jax.shard_map(
        shards, mesh=mesh, in_specs=placed, out_specs=P(("dp", "expert"), None), check_vma=False
    )
```
